128 devices in a mesh: dp: 4 (over z_lo, core), axial: 32 (over x, y, z_hi).
Axes of the slice: x: 4, y: 4, z: 4 (z_hi: 2, z_lo: 2; z = z_hi * 2 + z_lo), core: 2. Of those that a mesh axis runs over, the one named last changes fastest.
Arguments:
- pair_act: bfloat16 [2560, 640, 128], P(('dp', 'axial')), parts along dimension 0, may hold values from -6 to 6
- ln_gain: float32 [128], replicated, may hold values from 0.25 to 1.75
- ln_shift: float32 [128], replicated, may hold values from -3 to 3
- w_qkv: bfloat16 [128, 384], replicated, as said below
- w_bias: bfloat16 [128, 4], replicated, as said below
- w_gate: bfloat16 [128, 128], replicated, may hold values from -0.5 to 0.5
- gate_shift: float32 [128], replicated, may hold values from -4 to 4
- w_out: bfloat16 [128, 128], replicated, may hold values from -0.5 to 0.5
- out_shift: float32 [128], replicated, may hold values from -3 to 3
Outputs:
- updated: bfloat16 [2560, 640, 128], P(('dp', 'axial')), parts along dimension 0
The draws below stay inside these ranges and needn't reach their ends.
There are 4 independent parts, one for each index of `dp`. The reference program is written for one: setup_inputs(seed, part) draws one part's arguments, and reference() takes and returns one part's arrays. A program takes and returns all parts, laid end to end along the dimension named above; an argument that names none is the same for every part. Nothing has to cross between parts.
Inputs may be any that keep to these rules, and one draw needn't show every extreme that they name: `w_bias`: to one bias per head. `w_qkv`: keys and values.
All inputs are finite; a program needn't handle non-finite values.
Results may differ from the reference program's by a relative error of at most 0.0014.
The reference program's roundings to bfloat16 on the way (of `normed`, `bias`, `weights`, `attended` and `gated`) count: a program that leaves them out, or rounds other values in their place, can miss the bound.
Values may be sent and summed in bfloat16 or wider, within the bound.
A program may use at most 128 MiB of HBM per device.

```python
import jax
import jax.numpy as jnp
from jax import lax

CH = 128
HEADS = 4
HDIM = 32
HC = 128
NRES = 640


def draw_w_bias(key, part):
    key = jax.random.fold_in(key, 7)
    noise = jnp.clip(jax.random.normal(key, (CH, HEADS), jnp.float32), -4.0, 4.0) * CH ** (-0.5)
    spread = jnp.full((HEADS,), 0.2, jnp.float32)
    return (noise * spread).astype(jnp.bfloat16)


def draw_w_qkv(key, part):
    key = jax.random.fold_in(key, 11)
    noise = jnp.clip(jax.random.normal(key, (CH, 3 * HC), jnp.float32), -4.0, 4.0) * CH ** (-0.5)
    factor = jnp.full((HEADS,), 1.6, jnp.float32)
    column_scale = jnp.concatenate([jnp.repeat(factor, HDIM), jnp.ones((2 * HC,), jnp.float32)])
    return (noise * column_scale).astype(jnp.bfloat16)


def block_levels(own_key, shape, pieces, least, top_value):
    level = 1.0
    for dim, blocks in pieces:
        draws = jax.random.uniform(jax.random.fold_in(jax.random.fold_in(own_key, 6), dim), (blocks,), jnp.float32, least / len(pieces), top_value / len(pieces))
        level = level * jnp.repeat(jnp.exp(draws), shape[dim] // blocks).reshape((-1,) + (1,) * (len(shape) - 1 - dim))
    return level


def scatter_about(key, shape, deviation, reach, pieces=(), dtype=jnp.bfloat16):
    entries = jax.random.normal(key, shape, jnp.float32) * deviation
    if len(pieces) > 0:
        entries = block_levels(key, shape, pieces, -0.22, 0.18) * entries
    return jnp.clip(entries, min=-reach, max=reach).astype(dtype)


def setup_inputs(seed: int = 0, part: int = 0) -> dict:
    streams_of = jax.random.split(jax.random.key(seed), 10)
    part_keys = jax.random.split(jax.random.fold_in(streams_of[9], part), 10)
    pair_act = scatter_about(part_keys[0], (NRES, NRES, CH), 1.0, 6.0, ((0, 32),))
    ln_gain = jnp.clip(1.0 + 0.15 * jax.random.normal(streams_of[1], (CH,), jnp.float32), 0.25, 1.75)
    ln_shift = scatter_about(streams_of[2], (CH,), 0.5, 3.0, (), jnp.float32)
    w_qkv = draw_w_qkv(jax.random.fold_in(streams_of[9], 71), part)
    w_bias = draw_w_bias(jax.random.fold_in(streams_of[9], 71), part)
    w_gate = scatter_about(streams_of[5], (CH, HC), CH ** -0.5, 0.5)
    gate_shift = scatter_about(streams_of[6], (HC,), 1.0, 4.0, (), jnp.float32)
    w_out = scatter_about(streams_of[7], (HC, CH), HC ** -0.5, 0.5)
    out_shift = scatter_about(streams_of[8], (CH,), 0.5, 3.0, (), jnp.float32)
    return {"pair_act": pair_act, "ln_gain": ln_gain, "ln_shift": ln_shift, "w_qkv": w_qkv, "w_bias": w_bias, "w_gate": w_gate, "gate_shift": gate_shift, "w_out": w_out, "out_shift": out_shift}


def normalize(pair_act, ln_gain, ln_shift):
    values = pair_act.astype(jnp.float32)
    center = lax.optimization_barrier(jnp.mean(values, axis=-1, keepdims=True))
    spread = lax.optimization_barrier(jnp.mean((values - center) ** 2, axis=-1, keepdims=True))
    return ((values - center) * lax.rsqrt(spread + 1e-05) * ln_gain + ln_shift).astype(jnp.bfloat16)

def reference(pair_act, ln_gain, ln_shift, w_qkv, w_bias, w_gate, gate_shift, w_out, out_shift):
    normed = normalize(pair_act, ln_gain, ln_shift)
    flat = normed.reshape(-1, CH)
    projected = jnp.dot(flat, w_qkv, preferred_element_type=jnp.float32)
    scaling = jnp.concatenate([jnp.full((HC,), HDIM ** (-0.5), jnp.float32), jnp.ones((2 * HC,), jnp.float32)])
    projected = (projected * scaling).astype(jnp.bfloat16).reshape(NRES, NRES, 3, HEADS, HDIM)
    queries = jnp.moveaxis(projected[:, :, 0], 1, 0)
    key_rows = jnp.moveaxis(projected[:, :, 1], 1, 0)
    value_rows = jnp.moveaxis(projected[:, :, 2], 1, 0)
    bias = jnp.einsum('kic,ch->hik', normed.astype(jnp.float32), w_bias.astype(jnp.float32)).astype(jnp.bfloat16)
    bias_wide = bias.astype(jnp.float32)

    def one_column(items):
        query_col, key_col, value_col = items
        scores = jnp.einsum('ihd,khd->hik', query_col.astype(jnp.float32), key_col.astype(jnp.float32)) + bias_wide
        weights = jax.nn.softmax(scores, axis=-1).astype(jnp.bfloat16)
        result = jnp.einsum('hik,khd->ihd', weights.astype(jnp.float32), value_col.astype(jnp.float32))
        return result.astype(jnp.bfloat16)
    attended = lax.map(one_column, (queries, key_rows, value_rows))
    attended = jnp.moveaxis(attended, 0, 1).reshape(-1, HC)
    gate = jax.nn.sigmoid(jnp.dot(flat, w_gate, preferred_element_type=jnp.float32) + gate_shift)
    gated = (gate * attended.astype(jnp.float32)).astype(jnp.bfloat16)
    result = jnp.dot(gated, w_out, preferred_element_type=jnp.float32) + out_shift
    result = result + pair_act.reshape(-1, CH).astype(jnp.float32)
    return result.astype(jnp.bfloat16).reshape(NRES, NRES, CH)
```

```python
import functools

import jax
import jax.numpy as jnp
from jax import lax
from jax.experimental import pallas as pl
from jax.experimental.pallas import tpu as pltpu
from jax.sharding import PartitionSpec as P

HEADS = 4
HDIM = 32
CH = 128
MESH = pl.DeviceIdType.MESH
F32 = jnp.float32
BF16 = jnp.bfloat16
NT = (((1,), (1,)), ((), ()))


def normalize(values, gain, shift):
    center = jnp.mean(values, axis=-1, keepdims=True)
    spread = jnp.mean((values - center) ** 2, axis=-1, keepdims=True)
    return (values - center) * lax.rsqrt(spread + 1e-05) * gain + shift


def upper_half(shape):
    return lax.broadcasted_iota(jnp.int32, shape, len(shape) - 2) < 4


def balanced_offsets():
    rest = [(x, y, z) for x in range(4) for y in range(4) for z in range(2) if x or y or z]

    def load(o):
        out = [0] * 6
        for axis, step in enumerate((o[0], o[1], 2 * o[2])):
            out[2 * axis] += step in (1, 2)
            out[2 * axis + 1] += step in (2, 3)
        return out

    total, order = [0] * 6, []
    while rest:
        def cost(o):
            new = [t + a for t, a in zip(total, load(o))]
            return max(new) * 100 + sum(n * n for n in new), -sum(load(o))
        best = min(rest, key=cost)
        rest.remove(best)
        order.append(best)
        total = [t + a for t, a in zip(total, load(best))]
    return order


OFFSETS = balanced_offsets()


def kernel(
    n, pair, gain, shift, wq_t, wk, wv_t, wbias_t, wgate, gate_shift, wout, out_shift, out,
    send_in, recv_in, send_out, recv_out, bias_send, bias_recv, bias_all,
    mix, normed, update, rows_bias, q_t, keys, v_t, att_t,
    ss_bias, rs_bias, ss_in, rs_in, ss_out, rs_out, local_sem,
):
    rows, full, _ = pair.shape
    groups = send_in.shape[0]
    block = 4 * rows
    wide = n * 4
    me = lax.axis_index("axial")
    x, y, z = me // 8, lax.rem(me // 2, 4), lax.rem(me, 2)

    def peer(o):
        return (lax.rem(x + o[0], 4) * 4 + lax.rem(y + o[1], 4)) * 2 + lax.rem(z + o[2], 2)

    def bias_row(k, _):
        normal = normalize(pair[k].astype(F32), gain[...], shift[...]).astype(BF16)
        line = lax.dot_general(wbias_t[...], normal, NT, preferred_element_type=F32)
        for h in range(HEADS):
            place = jnp.where(k < 16, h * 16 + k, 4 * h + 48 + k)
            rows_bias[pl.ds(place, 1), :] = line[h : h + 1, :]
        return 0

    lax.fori_loop(0, rows, bias_row, 0)
    bias_send[...] = rows_bias[...].astype(BF16)

    def assemble(g, _):
        top = upper_half((n // 2, 8, CH))
        for a in range(0, rows, 2):
            even = pair[a, pl.ds(pl.multiple_of(g * wide, wide), wide), :].astype(F32).reshape(n // 2, 8, CH)
            odd = pair[a + 1, pl.ds(pl.multiple_of(g * wide, wide), wide), :].astype(F32).reshape(n // 2, 8, CH)
            mix[:, 0, 4 * a : 4 * a + 8, :] = jnp.where(top, even, pltpu.roll(odd, 4, 1))
            mix[:, 1, 4 * a : 4 * a + 8, :] = jnp.where(top, pltpu.roll(even, 4, 1), odd)
        send_in[g] = mix[...].astype(BF16).reshape(n, block, CH)
        return 0

    lax.fori_loop(0, groups, assemble, 0)

    barrier = pltpu.get_barrier_semaphore()
    for o in OFFSETS:
        pl.semaphore_signal(barrier, inc=1, device_id={"axial": peer(o)}, device_id_type=MESH)
    pl.semaphore_wait(barrier, n - 1)

    def remote(src, dst, ss, rs, to):
        return pltpu.make_async_remote_copy(
            src_ref=src, dst_ref=dst, send_sem=ss, recv_sem=rs, device_id={"axial": to}, device_id_type=MESH
        )

    def wait_bytes(ref, sem):
        pltpu.make_async_copy(ref, ref, sem).wait()

    for o in OFFSETS:
        remote(bias_send, bias_recv.at[me], ss_bias, rs_bias, peer(o)).start()
    own_bias = pltpu.make_async_copy(bias_send, bias_recv.at[me], local_sem.at[0])
    own_bias.start()

    def send_group(g, _):
        for o in OFFSETS:
            to = peer(o)
            remote(send_in.at[g, to], recv_in.at[g, me], ss_in.at[g], rs_in.at[g], to).start()
        pltpu.make_async_copy(send_in.at[g, me], recv_in.at[g, me], rs_in.at[g]).start()
        return 0

    lax.fori_loop(0, groups, send_group, 0)

    own_bias.wait()
    wait_bytes(bias_recv.at[pl.ds(0, n - 1)], rs_bias)

    def spread_bias(p, _):
        top = upper_half((8, full))
        turn = lambda tile: pltpu.roll(tile, 4, 0)
        first = bias_recv[2 * p].astype(F32)
        second = bias_recv[2 * p + 1].astype(F32)
        for h in range(HEADS):
            tail = slice(64 + h // 2 * 8, 72 + h // 2 * 8)
            first_tail, second_tail = first[tail], second[tail]
            if h % 2:
                first_tail = turn(first_tail)
            else:
                second_tail = turn(second_tail)
            low, high = turn(second[16 * h : 16 * h + 8]), turn(second[16 * h + 8 : 16 * h + 16])
            start = pl.multiple_of(2 * rows * p, 8)
            bias_all[h, pl.ds(start, 16), :] = first[16 * h : 16 * h + 16]
            bias_all[h, pl.ds(pl.multiple_of(start + 16, 8), 8), :] = jnp.where(top, first_tail, low)
            bias_all[h, pl.ds(pl.multiple_of(start + 24, 8), 8), :] = jnp.where(top, low, high)
            bias_all[h, pl.ds(pl.multiple_of(start + 32, 8), 8), :] = jnp.where(top, high, second_tail)
        return 0

    lax.fori_loop(0, n // 2, spread_bias, 0)

    def group(g, _):
        wait_bytes(recv_in.at[g], rs_in.at[g])

        def norm_block(s, _):
            values = recv_in[g, pl.ds(4 * s, 4)].astype(F32).reshape(4 * block, CH)
            normed[pl.ds(pl.multiple_of(4 * block * s, 4 * block), 4 * block), :] = normalize(
                values, gain[...], shift[...]
            )
            return 0

        lax.fori_loop(0, n // 4, norm_block, 0)

        def column(b, _):
            normal = normed[pl.ds(b, full, stride=4), :].astype(BF16)
            queries = lax.dot_general(wq_t[...], normal, NT, preferred_element_type=F32)
            q_t[...] = (queries * HDIM ** (-0.5)).astype(BF16)
            keys[...] = jnp.dot(normal, wk[...], preferred_element_type=F32).astype(BF16)
            v_t[...] = lax.dot_general(wv_t[...], normal, NT, preferred_element_type=F32).astype(BF16)
            gate = jax.nn.sigmoid(jnp.dot(normal, wgate[...], preferred_element_type=F32) + gate_shift[...])

            def head(h, _):
                mine = lax.broadcasted_iota(jnp.int32, (CH, full), 0) // HDIM == h
                query = jnp.where(mine, q_t[...], jnp.zeros((), BF16))
                scores = jnp.dot(keys[...], query, preferred_element_type=F32) + bias_all[h]
                top = jnp.max(scores, axis=0, keepdims=True)
                raised = jnp.exp(scores - top)
                weights = (raised * (1.0 / jnp.sum(raised, axis=0, keepdims=True))).astype(BF16)
                own = pl.ds(pl.multiple_of(h * HDIM, HDIM), HDIM)
                att_t[own, :] = jnp.dot(v_t[own, :], weights, preferred_element_type=F32)
                return 0

            lax.fori_loop(0, HEADS, head, 0)
            attended = att_t[...].T.astype(BF16).astype(F32)
            gated = (gate * attended).astype(BF16)
            update[pl.ds(b, full, stride=4), :] = (
                jnp.dot(gated, wout[...], preferred_element_type=F32) + out_shift[...]
            )
            return 0

        lax.fori_loop(0, 4, column, 0)

        def finish(s, _):
            values = recv_in[g, pl.ds(4 * s, 4)].astype(F32)
            total = update[pl.ds(pl.multiple_of(4 * block * s, 4 * block), 4 * block), :].reshape(4, block, CH) + values
            send_out[g, pl.ds(4 * s, 4)] = total.astype(BF16)
            return 0

        lax.fori_loop(0, n // 4, finish, 0)
        for o in OFFSETS:
            to = peer(o)
            remote(send_out.at[g, to], recv_out.at[g, me], ss_out.at[g], rs_out.at[g], to).start()
        pltpu.make_async_copy(send_out.at[g, me], recv_out.at[g, me], rs_out.at[g]).start()
        return 0

    lax.fori_loop(0, groups, group, 0)

    def collect(g, _):
        wait_bytes(recv_out.at[g], rs_out.at[g])
        top = upper_half((n // 2, 8, CH))
        mix[...] = recv_out[g].astype(F32).reshape(n // 2, 2, block, CH)
        for a in range(0, rows, 2):
            first = mix[:, 0, 4 * a : 4 * a + 8, :]
            second = mix[:, 1, 4 * a : 4 * a + 8, :]
            even = jnp.where(top, first, pltpu.roll(second, 4, 1))
            odd = jnp.where(top, pltpu.roll(first, 4, 1), second)
            here = pl.ds(pl.multiple_of(g * wide, wide), wide)
            out[a, here, :] = even.reshape(wide, CH).astype(BF16)
            out[a + 1, here, :] = odd.reshape(wide, CH).astype(BF16)
        return 0

    lax.fori_loop(0, groups, collect, 0)

    wait_bytes(bias_recv.at[pl.ds(0, n - 1)], ss_bias)

    def drain(g, _):
        wait_bytes(send_in.at[g, pl.ds(0, n - 1)], ss_in.at[g])
        wait_bytes(send_out.at[g, pl.ds(0, n - 1)], ss_out.at[g])
        return 0

    lax.fori_loop(0, groups, drain, 0)


def on_device(n, pair_act, ln_gain, ln_shift, w_qkv, w_bias, w_gate, gate_shift, w_out, out_shift):
    rows, full, channels = pair_act.shape
    groups = full // (4 * n)
    block = 4 * rows
    wbias_t = jnp.concatenate([w_bias.T, jnp.zeros((16 - HEADS, channels), BF16)], axis=0)
    vmem = pl.BlockSpec(memory_space=pltpu.VMEM)
    dma = pltpu.SemaphoreType.DMA
    return pl.pallas_call(
        functools.partial(kernel, n),
        out_shape=jax.ShapeDtypeStruct(pair_act.shape, BF16),
        in_specs=[vmem] * 11,
        out_specs=vmem,
        scratch_shapes=[
            pltpu.VMEM((groups, n, block, CH), BF16),
            pltpu.VMEM((groups, n, block, CH), BF16),
            pltpu.VMEM((groups, n, block, CH), BF16),
            pltpu.VMEM((groups, n, block, CH), BF16),
            pltpu.VMEM((HEADS * rows, full), BF16),
            pltpu.VMEM((n, HEADS * rows, full), BF16),
            pltpu.VMEM((HEADS, full, full), F32),
            pltpu.VMEM((n // 2, 2, block, CH), F32),
            pltpu.VMEM((n * block, CH), F32),
            pltpu.VMEM((n * block, CH), F32),
            pltpu.VMEM((HEADS * rows, full), F32),
            pltpu.VMEM((CH, full), BF16),
            pltpu.VMEM((full, CH), BF16),
            pltpu.VMEM((CH, full), BF16),
            pltpu.VMEM((CH, full), F32),
            dma, dma, dma((groups,)), dma((groups,)), dma((groups,)), dma((groups,)), dma((1,)),
        ],
        compiler_params=pltpu.CompilerParams(
            collective_id=0, has_side_effects=True, vmem_limit_bytes=58 * 2**20
        ),
        name="triangle",
    )(
        pair_act, ln_gain[None], ln_shift[None], w_qkv[:, :CH].T, w_qkv[:, CH : 2 * CH], w_qkv[:, 2 * CH :].T,
        wbias_t, w_gate, gate_shift[None], w_out, out_shift[None],
    )


def solution(mesh):
    in_specs = (P(("dp", "axial"), None, None), P(), P(), P(), P(), P(), P(), P(), P())
    out_specs = P(("dp", "axial"), None, None)
    return jax.shard_map(
        functools.partial(on_device, mesh.shape["axial"]),
        mesh=mesh, in_specs=in_specs, out_specs=out_specs, check_vma=False,
    )
```

```python
import functools

import jax
import jax.numpy as jnp
from jax import lax
from jax.experimental import pallas as pl
from jax.experimental.pallas import tpu as pltpu
from jax.sharding import PartitionSpec as P

HEADS = 4
HDIM = 32
CH = 128
MESH = pl.DeviceIdType.MESH
F32 = jnp.float32
BF16 = jnp.bfloat16
NT = (((1,), (1,)), ((), ()))


def normalize(values, gain, shift):
    center = jnp.mean(values, axis=-1, keepdims=True)
    spread = jnp.mean((values - center) ** 2, axis=-1, keepdims=True)
    return (values - center) * lax.rsqrt(spread + 1e-05) * gain + shift


def upper_half(shape):
    return lax.broadcasted_iota(jnp.int32, shape, len(shape) - 2) < 4


def balanced_offsets():
    rest = [(x, y, z) for x in range(4) for y in range(4) for z in range(2) if x or y or z]

    def load(o):
        out = [0] * 6
        for axis, step in enumerate((o[0], o[1], 2 * o[2])):
            out[2 * axis] += step in (1, 2)
            out[2 * axis + 1] += step in (2, 3)
        return out

    total, order = [0] * 6, []
    while rest:
        def cost(o):
            new = [t + a for t, a in zip(total, load(o))]
            return max(new) * 100 + sum(n * n for n in new), -sum(load(o))
        best = min(rest, key=cost)
        rest.remove(best)
        order.append(best)
        total = [t + a for t, a in zip(total, load(best))]
    return order


OFFSETS = balanced_offsets()


def pieces(full, size):
    return [(r, min(size, full - r)) for r in range(0, full, size)]


def interleave(*plans):
    done, out = [0] * len(plans), []
    for _ in range(sum(map(len, plans))):
        i = min(
            (i for i in range(len(plans)) if done[i] < len(plans[i])),
            key=lambda i: (done[i] + 0.5) / len(plans[i]),
        )
        out.append(plans[i][done[i]])
        done[i] += 1
    return out


def kernel(
    n, pair, gain, shift, w_qkv, wbias_t, wgate, gate_shift, wout, out_shift, out,
    send_in, recv_in, send_out, recv_out, bias_recv, bias_all,
    mix, normed, update, rows_bias, wq_t, wv_t, queries, keys, v_t, gates, scores, raised, stats, attended,
    ss_bias, rs_bias, ss_in, rs_in, ss_out, rs_out,
):
    rows, full, _ = pair.shape
    groups = send_in.shape[0]
    block = 4 * rows
    wide = n * 4
    lanes = full // CH
    units = 4 * 2 * lanes
    me = lax.axis_index("axial")
    x, y, z = me // 8, lax.rem(me // 2, 4), lax.rem(me, 2)

    def peer(o):
        return (lax.rem(x + o[0], 4) * 4 + lax.rem(y + o[1], 4)) * 2 + lax.rem(z + o[2], 2)

    barrier = pltpu.get_barrier_semaphore()
    for o in OFFSETS:
        pl.semaphore_signal(barrier, inc=1, device_id={"axial": peer(o)}, device_id_type=MESH)

    def remote(src, dst, ss, rs, to):
        return pltpu.make_async_remote_copy(
            src_ref=src, dst_ref=dst, send_sem=ss, recv_sem=rs, device_id={"axial": to}, device_id_type=MESH
        )

    def wait_bytes(ref, sem):
        pltpu.make_async_copy(ref, ref, sem).wait()

    def assemble(g):
        top = upper_half((n // 2, 8, CH))
        here = pl.ds(pl.multiple_of(g * wide, wide), wide)
        for a in range(0, rows, 2):
            even = pair[a, here, :].astype(F32).reshape(n // 2, 8, CH)
            odd = pair[a + 1, here, :].astype(F32).reshape(n // 2, 8, CH)
            mix[:, 0, 4 * a : 4 * a + 8, :] = jnp.where(top, even, pltpu.roll(odd, 4, 1))
            mix[:, 1, 4 * a : 4 * a + 8, :] = jnp.where(top, pltpu.roll(even, 4, 1), odd)
        send_in[g] = mix[...].astype(BF16).reshape(n, block, CH)

    def send_group(src, dst, ss, rs, g):
        for o in OFFSETS:
            to = peer(o)
            remote(src.at[g, to], dst.at[g, me], ss.at[g], rs.at[g], to).start()
        pltpu.make_async_copy(src.at[g, me], dst.at[g, me], rs.at[g]).start()

    assemble(0)
    pl.semaphore_wait(barrier, n - 1)
    send_group(send_in, recv_in, ss_in, rs_in, 0)

    def bias_row(k, _):
        normal = normalize(pair[k].astype(F32), gain[...], shift[...]).astype(BF16)
        line = lax.dot_general(wbias_t[...], normal, NT, preferred_element_type=F32)
        for h in range(HEADS):
            place = jnp.where(k < 16, h * 16 + k, 4 * h + 48 + k)
            rows_bias[pl.ds(place, 1), :] = line[h : h + 1, :]
        return 0

    lax.fori_loop(0, rows, bias_row, 0)
    bias_recv[x, y, z] = rows_bias[...].astype(BF16)

    first, second, third = slice(0, 32), slice(32, 64), slice(64, 80)
    every = slice(None)
    three = slice(0, 3)
    to_x = [(1, 0, 0), (3, 0, 0), (2, 0, 0)]
    to_y = [(0, 1, 0), (0, 3, 0), (0, 2, 0)]
    to_z = [(0, 0, 1)]
    waves = [
        [((x, y, z, first), to_z, (0, 0, 0, first)), ((x, y, z, second), to_x, (three, 0, 0, second)),
         ((x, y, z, third), to_y, (0, three, 0, third))],
        [((x, y, every, first), to_y, (0, three, every, first)), ((every, y, z, second), to_z, (every, 0, 0, second)),
         ((x, every, z, third), to_x, (three, every, 0, third))],
        [((x, every, every, first), to_x, (three, every, every, first)),
         ((every, y, every, second), to_y, (every, three, every, second)),
         ((every, every, z, third), to_z, (every, every, 0, third))],
    ]

    def start_wave(w):
        for p, (part, targets, _) in enumerate(waves[w]):
            for o in targets:
                remote(bias_recv.at[part], bias_recv.at[part], ss_bias.at[3 * w + p], rs_bias.at[3 * w + p], peer(o)).start()

    def wait_wave(w, sems):
        for p, (_, _, size) in enumerate(waves[w]):
            wait_bytes(bias_recv.at[size], sems.at[3 * w + p])

    start_wave(0)

    def rest(g, _):
        assemble(g)
        return 0

    lax.fori_loop(1, groups, rest, 0)
    wq_t[...] = w_qkv[:, 0:CH].astype(F32).T.astype(BF16)
    wv_t[...] = w_qkv[:, 2 * CH :].astype(F32).T.astype(BF16)
    queries[...] = jnp.zeros(queries.shape, BF16)
    wait_wave(0, rs_bias)
    start_wave(1)
    wait_wave(1, rs_bias)
    start_wave(2)

    def send_rest(g, _):
        send_group(send_in, recv_in, ss_in, rs_in, g)
        return 0

    lax.fori_loop(1, groups, send_rest, 0)

    def spread_bias(p, _):
        top = upper_half((8, full))
        turn = lambda tile: pltpu.roll(tile, 4, 0)
        px, py = p // 4, lax.rem(p, 4)
        even = bias_recv[px, py, 0].astype(F32)
        odd = bias_recv[px, py, 1].astype(F32)
        for h in range(HEADS):
            tail = slice(64 + h // 2 * 8, 72 + h // 2 * 8)
            even_tail, odd_tail = even[tail], odd[tail]
            if h % 2:
                even_tail = turn(even_tail)
            else:
                odd_tail = turn(odd_tail)
            low, high = turn(odd[16 * h : 16 * h + 8]), turn(odd[16 * h + 8 : 16 * h + 16])
            tiles = [
                even[16 * h : 16 * h + 8], even[16 * h + 8 : 16 * h + 16], jnp.where(top, even_tail, low),
                jnp.where(top, low, high), jnp.where(top, high, odd_tail),
            ]
            for k, tile in enumerate(tiles):
                start = pl.multiple_of(2 * rows * p + 8 * k, 8)
                for i in range(lanes):
                    bias_all[h // 2 * lanes + i, pl.ds(start, 8), h % 2 * CH : (h % 2 + 1) * CH] = tile[
                        :, i * CH : (i + 1) * CH
                    ]
        return 0

    def prepare(g):
        wait_bytes(recv_in.at[g], rs_in.at[g])

        def norm_block(s, _):
            values = recv_in[g, pl.ds(4 * s, 4)].astype(F32).reshape(4 * block, CH)
            normed[pl.ds(pl.multiple_of(4 * block * s, 4 * block), 4 * block), :] = normalize(
                values, gain[...], shift[...]
            )
            return 0

        lax.fori_loop(0, n // 4, norm_block, 0)

        def column(b, _):
            normal = normed[pl.ds(b, full, stride=4), :].astype(BF16)
            query = lax.dot_general(wq_t[...], normal, NT, preferred_element_type=F32)
            query = (query * HDIM ** (-0.5)).astype(BF16)
            for h in range(HEADS):
                own = slice(h * HDIM, (h + 1) * HDIM)
                for i in range(lanes):
                    queries[(b * 2 + h // 2) * lanes + i, own, h % 2 * CH : (h % 2 + 1) * CH] = query[
                        own, i * CH : (i + 1) * CH
                    ]
            keys[b] = jnp.dot(normal, w_qkv[:, CH : 2 * CH], preferred_element_type=F32).astype(BF16)
            v_t[b] = lax.dot_general(wv_t[...], normal, NT, preferred_element_type=F32).astype(BF16)
            gates[b] = jax.nn.sigmoid(jnp.dot(normal, wgate[...], preferred_element_type=F32) + gate_shift[...])
            return 0

        lax.fori_loop(0, 4, column, 0)

    plan = interleave(
        [(3, *c) for c in pieces(full, 128)], [(2, *c) for c in pieces(full, 128)], [(1, *c) for c in pieces(full, 320)]
    )

    def attend():
        def unit(t, slot):
            t1, t3 = jnp.minimum(t, units - 1), jnp.clip(t - 2, 0, units - 1)
            column1, place1 = t1 // (2 * lanes), lax.rem(t1, 2 * lanes)
            column3, place3 = t3 // (2 * lanes), lax.rem(t3, 2 * lanes)
            heads3, lane3 = pl.multiple_of(place3 // lanes * 2 * HDIM, 2 * HDIM), lax.rem(place3, lanes)
            query = queries[t1]
            top = jnp.max(stats[1 - slot, 0:8, :], axis=0, keepdims=True)
            share = 1.0 / jnp.sum(stats[slot, 8:16, :], axis=0, keepdims=True)
            most = jnp.full((8, 2 * CH), -jnp.inf, F32)
            total = jnp.zeros((8, 2 * CH), F32)
            result = jnp.zeros((2 * HDIM, 2 * CH), F32)
            for step, r, size in plan:
                here = slice(r, r + size)
                if step == 1:
                    score = jnp.dot(keys[column1, here, :], query, preferred_element_type=F32) + bias_all[place1, here, :]
                    scores[slot, here, :] = score
                    most = jnp.maximum(most, jnp.max(score.reshape(size // 8, 8, 2 * CH), axis=0))
                elif step == 2:
                    power = jnp.exp(scores[1 - slot, here, :] - top)
                    raised[1 - slot, here, :] = power
                    total = total + jnp.sum(power.reshape(size // 8, 8, 2 * CH), axis=0)
                else:
                    weights = (raised[slot, here, :] * share).astype(BF16)
                    result = result + jnp.dot(
                        v_t[column3, pl.ds(heads3, 2 * HDIM), here], weights, preferred_element_type=F32
                    )
            stats[slot, 0:8, :] = most
            stats[1 - slot, 8:16, :] = total
            attended[column3, lane3, pl.ds(heads3, HDIM), :] = result[0:HDIM, 0:CH]
            attended[column3, lane3, pl.ds(heads3 + HDIM, HDIM), :] = result[HDIM : 2 * HDIM, CH : 2 * CH]

        def two(u, _):
            unit(2 * u, 0)
            unit(2 * u + 1, 1)
            return 0

        lax.fori_loop(0, units // 2 + 1, two, 0)

    def conclude(g):
        def column(b, _):
            for i in range(lanes):
                rounded = attended[b, i].T.astype(BF16).astype(F32)
                gated = (gates[b, i * CH : (i + 1) * CH, :] * rounded).astype(BF16)
                update[pl.ds(b + 4 * CH * i, CH, stride=4), :] = (
                    jnp.dot(gated, wout[...], preferred_element_type=F32) + out_shift[...]
                )
            return 0

        lax.fori_loop(0, 4, column, 0)

        def finish(s, _):
            values = recv_in[g, pl.ds(4 * s, 4)].astype(F32)
            here = pl.ds(pl.multiple_of(4 * block * s, 4 * block), 4 * block)
            send_out[g, pl.ds(4 * s, 4)] = (update[here, :].reshape(4, block, CH) + values).astype(BF16)
            return 0

        lax.fori_loop(0, n // 4, finish, 0)
        send_group(send_out, recv_out, ss_out, rs_out, g)

    prepare(0)
    wait_wave(2, rs_bias)
    lax.fori_loop(0, n // 2, spread_bias, 0)

    def group(g, _):
        attend()
        conclude(g)

        @pl.when(g < groups - 1)
        def _():
            prepare(g + 1)

        return 0

    lax.fori_loop(0, groups, group, 0)

    def collect(g, _):
        wait_bytes(recv_out.at[g], rs_out.at[g])
        top = upper_half((n // 2, 8, CH))
        mix[...] = recv_out[g].astype(F32).reshape(n // 2, 2, block, CH)
        for a in range(0, rows, 2):
            low = mix[:, 0, 4 * a : 4 * a + 8, :]
            high = mix[:, 1, 4 * a : 4 * a + 8, :]
            even = jnp.where(top, low, pltpu.roll(high, 4, 1))
            odd = jnp.where(top, pltpu.roll(low, 4, 1), high)
            here = pl.ds(pl.multiple_of(g * wide, wide), wide)
            out[a, here, :] = even.reshape(wide, CH).astype(BF16)
            out[a + 1, here, :] = odd.reshape(wide, CH).astype(BF16)
        return 0

    lax.fori_loop(0, groups, collect, 0)

    for w in range(3):
        wait_wave(w, ss_bias)

    def drain(g, _):
        wait_bytes(send_in.at[g, pl.ds(0, n - 1)], ss_in.at[g])
        wait_bytes(send_out.at[g, pl.ds(0, n - 1)], ss_out.at[g])
        return 0

    lax.fori_loop(0, groups, drain, 0)


def on_device(n, pair_act, ln_gain, ln_shift, w_qkv, w_bias, w_gate, gate_shift, w_out, out_shift):
    rows, full, channels = pair_act.shape
    groups = full // (4 * n)
    block = 4 * rows
    lanes = full // CH
    wbias_t = jnp.concatenate([w_bias.T, jnp.zeros((16 - HEADS, channels), BF16)], axis=0)
    vmem = pl.BlockSpec(memory_space=pltpu.VMEM)
    dma = pltpu.SemaphoreType.DMA
    return pl.pallas_call(
        functools.partial(kernel, n),
        out_shape=jax.ShapeDtypeStruct(pair_act.shape, BF16),
        in_specs=[vmem] * 9,
        out_specs=vmem,
        scratch_shapes=[
            pltpu.VMEM((groups, n, block, CH), BF16),
            pltpu.VMEM((groups, n, block, CH), BF16),
            pltpu.VMEM((groups, n, block, CH), BF16),
            pltpu.VMEM((groups, n, block, CH), BF16),
            pltpu.VMEM((4, 4, 2, HEADS * rows, full), BF16),
            pltpu.VMEM((2 * lanes, full, 2 * CH), F32),
            pltpu.VMEM((n // 2, 2, block, CH), F32),
            pltpu.VMEM((n * block, CH), F32),
            pltpu.VMEM((n * block, CH), F32),
            pltpu.VMEM((HEADS * rows, full), F32),
            pltpu.VMEM((CH, CH), BF16),
            pltpu.VMEM((CH, CH), BF16),
            pltpu.VMEM((8 * lanes, CH, 2 * CH), BF16),
            pltpu.VMEM((4, full, CH), BF16),
            pltpu.VMEM((4, CH, full), BF16),
            pltpu.VMEM((4, full, CH), F32),
            pltpu.VMEM((2, full, 2 * CH), F32),
            pltpu.VMEM((2, full, 2 * CH), F32),
            pltpu.VMEM((2, 16, 2 * CH), F32),
            pltpu.VMEM((4, lanes, CH, CH), F32),
            dma((9,)), dma((9,)), dma((groups,)), dma((groups,)), dma((groups,)), dma((groups,)),
        ],
        compiler_params=pltpu.CompilerParams(
            collective_id=0, has_side_effects=True, vmem_limit_bytes=54 * 2**20
        ),
        name="triangle",
    )(
        pair_act, ln_gain[None], ln_shift[None], w_qkv, wbias_t, w_gate, gate_shift[None], w_out, out_shift[None],
    )


def solution(mesh):
    in_specs = (P(("dp", "axial"), None, None), P(), P(), P(), P(), P(), P(), P(), P())
    out_specs = P(("dp", "axial"), None, None)
    return jax.shard_map(
        functools.partial(on_device, mesh.shape["axial"]),
        mesh=mesh, in_specs=in_specs, out_specs=out_specs, check_vma=False,
    )
```

```python
import functools

import jax
import jax.numpy as jnp
from jax import lax
from jax.experimental import pallas as pl
from jax.experimental.pallas import tpu as pltpu
from jax.sharding import PartitionSpec as P

HEADS = 4
HDIM = 32
CH = 128
LOG2E = 1.4426950408889634
MESH = pl.DeviceIdType.MESH
F32 = jnp.float32
BF16 = jnp.bfloat16
NT = (((1,), (1,)), ((), ()))


def normalize(values, gain, shift):
    center = jnp.mean(values, axis=-1, keepdims=True)
    spread = jnp.mean((values - center) ** 2, axis=-1, keepdims=True)
    return (values - center) * lax.rsqrt(spread + 1e-05) * gain + shift


def upper_half(shape):
    return lax.broadcasted_iota(jnp.int32, shape, len(shape) - 2) < 4


def balanced_offsets():
    rest = [(x, y, z) for x in range(4) for y in range(4) for z in range(2) if x or y or z]

    def load(o):
        out = [0] * 6
        for axis, step in enumerate((o[0], o[1], 2 * o[2])):
            out[2 * axis] += step in (1, 2)
            out[2 * axis + 1] += step in (2, 3)
        return out

    total, order = [0] * 6, []
    while rest:
        def cost(o):
            new = [t + a for t, a in zip(total, load(o))]
            return max(new) * 100 + sum(n * n for n in new), -sum(load(o))
        best = min(rest, key=cost)
        rest.remove(best)
        order.append(best)
        total = [t + a for t, a in zip(total, load(best))]
    return order


OFFSETS = balanced_offsets()


def pieces(full, size):
    return [(r, min(size, full - r)) for r in range(0, full, size)]


def interleave(*plans):
    done, out = [0] * len(plans), []
    for _ in range(sum(map(len, plans))):
        i = min(
            (i for i in range(len(plans)) if done[i] < len(plans[i])),
            key=lambda i: (done[i] + 0.5) / len(plans[i]),
        )
        out.append(plans[i][done[i]])
        done[i] += 1
    return out


def kernel(
    n, pair, gain, shift, w_qkv, w_bias, wgate, gate_shift, wout, out_shift, out,
    send_in, recv_in, send_out, recv_out, bias_recv, bias_all,
    mix, normed, update, rows_bias, wq_t, wk_twice, wv_t, queries, keys, v_t, gates, scores, raised, stats, attended,
    ss_bias, rs_bias, ss_in, rs_in, ss_out, rs_out,
):
    rows, full, _ = pair.shape
    groups = send_in.shape[0]
    block = 4 * rows
    wide = n * 4
    lanes = full // CH
    units = 4 * 2 * lanes
    me = lax.axis_index("axial")
    x, y, z = me // 8, lax.rem(me // 2, 4), lax.rem(me, 2)

    def peer(o):
        return (lax.rem(x + o[0], 4) * 4 + lax.rem(y + o[1], 4)) * 2 + lax.rem(z + o[2], 2)

    barrier = pltpu.get_barrier_semaphore()
    for o in OFFSETS:
        pl.semaphore_signal(barrier, inc=1, device_id={"axial": peer(o)}, device_id_type=MESH)

    def remote(src, dst, ss, rs, to):
        return pltpu.make_async_remote_copy(
            src_ref=src, dst_ref=dst, send_sem=ss, recv_sem=rs, device_id={"axial": to}, device_id_type=MESH
        )

    def chunk(d):
        return pl.ds(pl.multiple_of(d * block, block), block)

    def wait_bytes(ref, sem):
        pltpu.make_async_copy(ref, ref, sem).wait()

    def assemble(g):
        top = upper_half((n // 2, 8, CH))
        here = pl.ds(pl.multiple_of(g * wide, wide), wide)
        for a in range(0, rows, 2):
            even = pair[a, here, :].astype(F32).reshape(n // 2, 8, CH)
            odd = pair[a + 1, here, :].astype(F32).reshape(n // 2, 8, CH)
            mix[:, 0, 4 * a : 4 * a + 8, :] = jnp.where(top, even, pltpu.roll(odd, 4, 1))
            mix[:, 1, 4 * a : 4 * a + 8, :] = jnp.where(top, pltpu.roll(even, 4, 1), odd)
        send_in[g] = mix[...].astype(BF16).reshape(n * block, CH)

    def send_group(src, dst, ss, rs, g):
        for o in OFFSETS:
            to = peer(o)
            remote(src.at[g, chunk(to)], dst.at[g, chunk(me)], ss.at[g], rs.at[g], to).start()
        pltpu.make_async_copy(src.at[g, chunk(me)], dst.at[g, chunk(me)], rs.at[g]).start()

    wbias_t = w_bias[...]

    def bias_rows(k4, _):
        for k in range(4):
            normal = normalize(pair[4 * k4 + k].astype(F32), gain[...], shift[...]).astype(BF16)
            line = lax.dot_general(wbias_t, normal, NT, preferred_element_type=F32)
            for h in range(HEADS):
                place = jnp.where(k4 < 4, h * 16 + 4 * k4, 4 * h + 64) + k
                rows_bias[pl.ds(place, 1), :] = line[h : h + 1, :]
        return 0

    lax.fori_loop(0, rows // 4, bias_rows, 0)
    bias_recv[x, y, z] = rows_bias[...].astype(BF16)

    first, second, third = slice(0, 32), slice(32, 64), slice(64, 80)
    every = slice(None)
    three = slice(0, 3)
    to_x = [(1, 0, 0), (3, 0, 0), (2, 0, 0)]
    to_y = [(0, 1, 0), (0, 3, 0), (0, 2, 0)]
    to_z = [(0, 0, 1)]
    waves = [
        [((x, y, z, first), to_z, (0, 0, 0, first)), ((x, y, z, second), to_x, (three, 0, 0, second)),
         ((x, y, z, third), to_y, (0, three, 0, third))],
        [((x, y, every, first), to_y, (0, three, every, first)), ((every, y, z, second), to_z, (every, 0, 0, second)),
         ((x, every, z, third), to_x, (three, every, 0, third))],
        [((x, every, every, first), to_x, (three, every, every, first)),
         ((every, y, every, second), to_y, (every, three, every, second)),
         ((every, every, z, third), to_z, (every, every, 0, third))],
    ]

    def start_wave(w):
        for p, (part, targets, _) in enumerate(waves[w]):
            for o in targets:
                remote(bias_recv.at[part], bias_recv.at[part], ss_bias.at[3 * w + p], rs_bias.at[3 * w + p], peer(o)).start()

    def wait_wave(w, sems):
        for p, (_, _, size) in enumerate(waves[w]):
            wait_bytes(bias_recv.at[size], sems.at[3 * w + p])

    pl.semaphore_wait(barrier, n - 1)
    start_wave(0)
    assemble(0)
    send_group(send_in, recv_in, ss_in, rs_in, 0)

    def rest(g, _):
        assemble(g)
        return 0

    lax.fori_loop(1, groups, rest, 0)
    wq_t[...] = w_qkv[:, 0:CH].astype(F32).T.astype(BF16)
    wk = w_qkv[:, CH : 2 * CH].astype(F32)
    swapped = pltpu.roll(wk, 2 * HDIM, 1)
    left = lax.broadcasted_iota(jnp.int32, (CH, CH), 1) < 2 * HDIM
    wk_twice[0] = jnp.where(left, wk, swapped).astype(BF16)
    wk_twice[1] = jnp.where(left, swapped, wk).astype(BF16)
    wv_t[...] = w_qkv[:, 2 * CH :].astype(F32).T.astype(BF16)
    queries[...] = jnp.zeros(queries.shape, BF16)
    wait_wave(0, rs_bias)
    start_wave(1)
    wait_wave(1, rs_bias)
    start_wave(2)

    def send_rest(g, _):
        send_group(send_in, recv_in, ss_in, rs_in, g)
        return 0

    lax.fori_loop(1, groups, send_rest, 0)

    def spread_bias(p, _):
        top = upper_half((8, full))
        turn = lambda tile: pltpu.roll(tile, 4, 0)
        px, py = p // 4, lax.rem(p, 4)
        even = bias_recv[px, py, 0].astype(F32) * LOG2E
        odd = bias_recv[px, py, 1].astype(F32) * LOG2E
        for h in range(HEADS):
            tail = slice(64 + h // 2 * 8, 72 + h // 2 * 8)
            even_tail, odd_tail = even[tail], odd[tail]
            if h % 2:
                even_tail = turn(even_tail)
            else:
                odd_tail = turn(odd_tail)
            low, high = turn(odd[16 * h : 16 * h + 8]), turn(odd[16 * h + 8 : 16 * h + 16])
            tiles = [
                even[16 * h : 16 * h + 8], even[16 * h + 8 : 16 * h + 16], jnp.where(top, even_tail, low),
                jnp.where(top, low, high), jnp.where(top, high, odd_tail),
            ]
            for k, tile in enumerate(tiles):
                start = pl.multiple_of(2 * rows * p + 8 * k, 8)
                for i in range(lanes):
                    bias_all[h // 2 * lanes + i, pl.ds(start, 8), h % 2 * CH : (h % 2 + 1) * CH] = tile[
                        :, i * CH : (i + 1) * CH
                    ]
        return 0

    def prepare(g):
        wait_bytes(recv_in.at[g], rs_in.at[g])

        def norm_block(s, _):
            here = pl.ds(pl.multiple_of(8 * block * s, 8 * block), 8 * block)
            normed[here, :] = normalize(recv_in[g, here, :].astype(F32), gain[...], shift[...])
            return 0

        lax.fori_loop(0, n // 8, norm_block, 0)

        def column(b):
            normal = normed[pl.ds(b, full, stride=4), :].astype(BF16)
            query = lax.dot_general(wq_t[...], normal, NT, preferred_element_type=F32)
            query = (query * HDIM ** (-0.5)).astype(BF16).astype(F32) * LOG2E
            high = query.astype(BF16)
            low = (query - high.astype(F32)).astype(BF16)
            for h in range(HEADS):
                own = slice(h * HDIM, (h + 1) * HDIM)
                for i in range(lanes):
                    unit, side, here = (b * 2 + h // 2) * lanes + i, h % 2 * CH, slice(i * CH, (i + 1) * CH)
                    row = h % 2 * HDIM
                    queries[unit, row : row + HDIM, side : side + CH] = high[own, here]
                    queries[unit, 2 * HDIM + row : 3 * HDIM + row, side : side + CH] = low[own, here]
            for p in range(2):
                keys[b, p] = jnp.dot(normal, wk_twice[p], preferred_element_type=F32).astype(BF16)
            v_t[b] = lax.dot_general(wv_t[...], normal, NT, preferred_element_type=F32).astype(BF16)
            gates[b] = jax.nn.sigmoid(jnp.dot(normal, wgate[...], preferred_element_type=F32) + gate_shift[...])

        def columns(b2, _):
            column(2 * b2)
            column(2 * b2 + 1)
            return 0

        lax.fori_loop(0, 2, columns, 0)

    plan = interleave(
        [(3, *c) for c in pieces(full, 128)], [(2, *c) for c in pieces(full, 128)], [(1, *c) for c in pieces(full, 320)]
    )

    def query_block(turn):
        return lax.rem(turn + me, lanes)

    def attend(g):
        def unit(t, slot):
            t1, t3 = jnp.minimum(t, units - 1), jnp.clip(t - 2, 0, units - 1)
            column1, heads1 = lax.rem(t1, 8) // 2, lax.rem(t1, 2)
            place1 = heads1 * lanes + query_block(t1 // 8)
            column3, lane3 = lax.rem(t3, 8) // 2, query_block(t3 // 8)
            heads3 = pl.multiple_of(lax.rem(t3, 2) * 2 * HDIM, 2 * HDIM)
            query = queries[column1 * 2 * lanes + place1]
            top = jnp.max(stats[1 - slot, 0:8, :], axis=0, keepdims=True)
            share = 1.0 / jnp.sum(stats[slot, 8:16, :], axis=0, keepdims=True)
            most = jnp.full((8, 2 * CH), -jnp.inf, F32)
            total = jnp.zeros((8, 2 * CH), F32)
            result = jnp.zeros((2 * HDIM, 2 * CH), F32)
            for step, r, size in plan:
                here = slice(r, r + size)
                if step == 1:
                    score = jnp.dot(keys[column1, heads1, here, :], query, preferred_element_type=F32) + bias_all[place1, here, :]
                    scores[slot, here, :] = score
                    most = jnp.maximum(most, jnp.max(score.reshape(size // 8, 8, 2 * CH), axis=0))
                elif step == 2:
                    power = jnp.exp2(scores[1 - slot, here, :] - top)
                    raised[1 - slot, here, :] = power
                    total = total + jnp.sum(power.reshape(size // 8, 8, 2 * CH), axis=0)
                else:
                    weights = (raised[slot, here, :] * share).astype(BF16)
                    result = result + jnp.dot(
                        v_t[column3, pl.ds(heads3, 2 * HDIM), here], weights, preferred_element_type=F32
                    )
            stats[slot, 0:8, :] = most
            stats[1 - slot, 8:16, :] = total
            attended[column3, lane3, pl.ds(heads3, HDIM), :] = result[0:HDIM, 0:CH]
            attended[column3, lane3, pl.ds(heads3 + HDIM, HDIM), :] = result[HDIM : 2 * HDIM, CH : 2 * CH]

        def two(u, _):
            unit(2 * u, 0)
            unit(2 * u + 1, 1)
            return 0

        def turn(i, _):
            two(4 * i, 0)

            @pl.when(i > 0)
            def _():
                conclude(g, i - 1)

            @pl.when(i < lanes)
            def _():
                lax.fori_loop(4 * i + 1, 4 * i + 4, two, 0)

            return 0

        lax.fori_loop(0, lanes + 1, turn, 0)

    def conclude(g, turn):
        i = query_block(turn)

        for b in range(4):
            rounded = attended[b, i].T.astype(BF16).astype(F32)
            gated = (gates[b, pl.ds(pl.multiple_of(i * CH, CH), CH), :] * rounded).astype(BF16)
            update[pl.ds(b, CH, stride=4), :] = jnp.dot(gated, wout[...], preferred_element_type=F32) + out_shift[...]
        here = pl.ds(pl.multiple_of(4 * CH * i, 4 * CH), 4 * CH)
        send_out[g, here, :] = (update[...] + recv_in[g, here, :].astype(F32)).astype(BF16)

        def give(s, _):
            @pl.when(s != me)
            def _():
                remote(send_out.at[g, chunk(s)], recv_out.at[g, chunk(me)], ss_out.at[g], rs_out.at[g], s).start()

            @pl.when(s == me)
            def _():
                pltpu.make_async_copy(send_out.at[g, chunk(s)], recv_out.at[g, chunk(s)], rs_out.at[g]).start()

            return 0

        least = (CH * i + rows - 1) // rows - jnp.where((turn > 0) & (i > 0), 1, 0)
        most = CH * (i + 1) // rows + jnp.where((turn == lanes - 1) & (i < lanes - 1), 1, 0)
        lax.fori_loop(least, most, give, 0)

    prepare(0)
    wait_wave(2, rs_bias)
    lax.fori_loop(0, n // 2, spread_bias, 0)

    def group(g, _):
        attend(g)

        @pl.when(g < groups - 1)
        def _():
            prepare(g + 1)

        return 0

    lax.fori_loop(0, groups, group, 0)

    def collect(g, _):
        wait_bytes(recv_out.at[g], rs_out.at[g])
        top = upper_half((n // 2, 8, CH))
        mix[...] = recv_out[g].astype(F32).reshape(n // 2, 2, block, CH)
        for a in range(0, rows, 2):
            low = mix[:, 0, 4 * a : 4 * a + 8, :]
            high = mix[:, 1, 4 * a : 4 * a + 8, :]
            even = jnp.where(top, low, pltpu.roll(high, 4, 1))
            odd = jnp.where(top, pltpu.roll(low, 4, 1), high)
            here = pl.ds(pl.multiple_of(g * wide, wide), wide)
            out[a, here, :] = even.reshape(wide, CH).astype(BF16)
            out[a + 1, here, :] = odd.reshape(wide, CH).astype(BF16)
        return 0

    lax.fori_loop(0, groups, collect, 0)

    for w in range(3):
        wait_wave(w, ss_bias)

    def drain(g, _):
        wait_bytes(send_in.at[g, pl.ds(0, (n - 1) * block)], ss_in.at[g])
        wait_bytes(send_out.at[g, pl.ds(0, (n - 1) * block)], ss_out.at[g])
        return 0

    lax.fori_loop(0, groups, drain, 0)


def on_device(n, pair_act, ln_gain, ln_shift, w_qkv, w_bias, w_gate, gate_shift, w_out, out_shift):
    rows, full, channels = pair_act.shape
    groups = full // (4 * n)
    block = 4 * rows
    lanes = full // CH
    vmem = pl.BlockSpec(memory_space=pltpu.VMEM)
    dma = pltpu.SemaphoreType.DMA
    return pl.pallas_call(
        functools.partial(kernel, n),
        out_shape=jax.ShapeDtypeStruct(pair_act.shape, BF16),
        in_specs=[vmem] * 9,
        out_specs=vmem,
        scratch_shapes=[
            pltpu.VMEM((groups, n * block, CH), BF16),
            pltpu.VMEM((groups, n * block, CH), BF16),
            pltpu.VMEM((groups, n * block, CH), BF16),
            pltpu.VMEM((groups, n * block, CH), BF16),
            pltpu.VMEM((4, 4, 2, HEADS * rows, full), BF16),
            pltpu.VMEM((2 * lanes, full, 2 * CH), F32),
            pltpu.VMEM((n // 2, 2, block, CH), F32),
            pltpu.VMEM((n * block, CH), F32),
            pltpu.VMEM((4 * CH, CH), F32),
            pltpu.VMEM((HEADS * rows, full), F32),
            pltpu.VMEM((CH, CH), BF16),
            pltpu.VMEM((2, CH, CH), BF16),
            pltpu.VMEM((CH, CH), BF16),
            pltpu.VMEM((8 * lanes, CH, 2 * CH), BF16),
            pltpu.VMEM((4, 2, full, CH), BF16),
            pltpu.VMEM((4, CH, full), BF16),
            pltpu.VMEM((4, full, CH), F32),
            pltpu.VMEM((2, full, 2 * CH), F32),
            pltpu.VMEM((2, full, 2 * CH), F32),
            pltpu.VMEM((2, 16, 2 * CH), F32),
            pltpu.VMEM((4, lanes, CH, CH), F32),
            dma((9,)), dma((9,)), dma((groups,)), dma((groups,)), dma((groups,)), dma((groups,)),
        ],
        compiler_params=pltpu.CompilerParams(
            collective_id=0, has_side_effects=True, vmem_limit_bytes=56 * 2**20
        ),
        name="triangle",
    )(
        pair_act, ln_gain[None], ln_shift[None], w_qkv, w_bias.T, w_gate, gate_shift[None], w_out, out_shift[None],
    )


def solution(mesh):
    in_specs = (P(("dp", "axial"), None, None), P(), P(), P(), P(), P(), P(), P(), P())
    out_specs = P(("dp", "axial"), None, None)
    return jax.shard_map(
        functools.partial(on_device, mesh.shape["axial"]),
        mesh=mesh, in_specs=in_specs, out_specs=out_specs, check_vma=False,
    )
```

```python
import functools

import jax
import jax.numpy as jnp
from jax import lax
from jax.experimental import pallas as pl
from jax.experimental.pallas import tpu as pltpu
from jax.sharding import PartitionSpec as P

HEADS = 4
HDIM = 32
CH = 128
LOG2E = 1.4426950408889634
MESH = pl.DeviceIdType.MESH
F32 = jnp.float32
BF16 = jnp.bfloat16
NT = (((1,), (1,)), ((), ()))


def normalize(values, gain, shift):
    center = jnp.mean(values, axis=-1, keepdims=True)
    spread = jnp.mean((values - center) ** 2, axis=-1, keepdims=True)
    return (values - center) * lax.rsqrt(spread + 1e-05) * gain + shift


def upper_half(shape):
    return lax.broadcasted_iota(jnp.int32, shape, len(shape) - 2) < 4


def balanced_offsets():
    rest = [(x, y, z) for x in range(4) for y in range(4) for z in range(2) if x or y or z]

    def load(o):
        out = [0] * 6
        for axis, step in enumerate((o[0], o[1], 2 * o[2])):
            out[2 * axis] += step in (1, 2)
            out[2 * axis + 1] += step in (2, 3)
        return out

    total, order = [0] * 6, []
    while rest:
        def cost(o):
            new = [t + a for t, a in zip(total, load(o))]
            return max(new) * 100 + sum(n * n for n in new), -sum(load(o))
        best = min(rest, key=cost)
        rest.remove(best)
        order.append(best)
        total = [t + a for t, a in zip(total, load(best))]
    return order


OFFSETS = balanced_offsets()


def pieces(full, size):
    return [(r, min(size, full - r)) for r in range(0, full, size)]


def interleave(*plans):
    done, out = [0] * len(plans), []
    for _ in range(sum(map(len, plans))):
        i = min(
            (i for i in range(len(plans)) if done[i] < len(plans[i])),
            key=lambda i: (done[i] + 0.5) / len(plans[i]),
        )
        out.append(plans[i][done[i]])
        done[i] += 1
    return out


def kernel(
    n, pair, gain, shift, w_qkv, w_bias, wgate, gate_shift, wout, out_shift, recv_out,
    send_in, recv_in, send_out, bias_recv, bias_all,
    mix, normed, update, rows_bias, wq_t, wk_twice, wv_t, queries, keys, v_t, gates, scores, raised, stats, attended,
    ss_bias, rs_bias, ss_in, rs_in, ss_out, rs_out,
):
    rows, full, _ = pair.shape
    groups = send_in.shape[0]
    block = 4 * rows
    wide = n * 4
    lanes = full // CH
    units = 4 * 2 * lanes
    me = lax.axis_index("axial")
    x, y, z = me // 8, lax.rem(me // 2, 4), lax.rem(me, 2)

    def peer(o):
        return (lax.rem(x + o[0], 4) * 4 + lax.rem(y + o[1], 4)) * 2 + lax.rem(z + o[2], 2)

    barrier = pltpu.get_barrier_semaphore()
    for o in OFFSETS:
        pl.semaphore_signal(barrier, inc=1, device_id={"axial": peer(o)}, device_id_type=MESH)

    def remote(src, dst, ss, rs, to):
        return pltpu.make_async_remote_copy(
            src_ref=src, dst_ref=dst, send_sem=ss, recv_sem=rs, device_id={"axial": to}, device_id_type=MESH
        )

    def chunk(d):
        return pl.ds(pl.multiple_of(d * block, block), block)

    def wait_bytes(ref, sem):
        pltpu.make_async_copy(ref, ref, sem).wait()

    def assemble(g):
        top = upper_half((n // 2, 8, CH))
        here = pl.ds(pl.multiple_of(g * wide, wide), wide)
        for a in range(0, rows, 2):
            even = pair[a, here, :].astype(F32).reshape(n // 2, 8, CH)
            odd = pair[a + 1, here, :].astype(F32).reshape(n // 2, 8, CH)
            mix[:, 0, 4 * a : 4 * a + 8, :] = jnp.where(top, even, pltpu.roll(odd, 4, 1))
            mix[:, 1, 4 * a : 4 * a + 8, :] = jnp.where(top, pltpu.roll(even, 4, 1), odd)
        send_in[g] = mix[...].astype(BF16).reshape(n * block, CH)

    def send_group(src, dst, ss, rs, g):
        for o in OFFSETS:
            to = peer(o)
            remote(src.at[g, chunk(to)], dst.at[g, chunk(me)], ss.at[g], rs.at[g], to).start()
        pltpu.make_async_copy(src.at[g, chunk(me)], dst.at[g, chunk(me)], rs.at[g]).start()

    wbias_t = w_bias[...]

    def bias_rows(k4, _):
        for k in range(4):
            normal = normalize(pair[4 * k4 + k].astype(F32), gain[...], shift[...]).astype(BF16)
            line = lax.dot_general(wbias_t, normal, NT, preferred_element_type=F32)
            for h in range(HEADS):
                place = jnp.where(k4 < 4, h * 16 + 4 * k4, 4 * h + 64) + k
                rows_bias[pl.ds(place, 1), :] = line[h : h + 1, :]
        return 0

    lax.fori_loop(0, rows // 4, bias_rows, 0)
    bias_recv[x, y, z] = rows_bias[...].astype(BF16)

    first, second, third = slice(0, 32), slice(32, 64), slice(64, 80)
    every = slice(None)
    three = slice(0, 3)
    lower, upper = slice(0, 2), slice(2, 4)
    before = lambda place: lax.rem(place + 3, 4)
    after = lambda place: lax.rem(place + 1, 4)
    to_x = [(1, 0, 0), (3, 0, 0), (2, 0, 0)]
    to_y = [(0, 1, 0), (0, 3, 0), (0, 2, 0)]
    to_z = [(0, 0, 1)]
    waves = [
        [((x, y, z, first), to_z, (0, 0, 0, first)), ((x, y, z, second), to_x, (three, 0, 0, second)),
         ((x, y, z, third), to_y, (0, three, 0, third))],
        [((x, y, every, first), to_y, (0, three, every, first)), ((every, y, z, second), to_z, (every, 0, 0, second)),
         ((x, every, z, third), to_x, (three, every, 0, third))],
        [((x, every, every, first), to_x[:2], (lower, every, every, first)),
         ((every, y, every, second), to_y[:2], (every, lower, every, second)),
         ((every, every, z, third), to_z, (every, every, 0, third))],
        [((before(x), lower, every, first), to_x[:1], (0, lower, every, first)),
         ((after(x), upper, every, first), to_x[1:2], (0, lower, every, first)),
         ((lower, before(y), every, second), to_y[:1], (lower, 0, every, second)),
         ((upper, after(y), every, second), to_y[1:2], (lower, 0, every, second))],
    ]

    def start_wave(w):
        for p, (part, targets, _) in enumerate(waves[w]):
            for o in targets:
                remote(bias_recv.at[part], bias_recv.at[part], ss_bias.at[4 * w + p], rs_bias.at[4 * w + p], peer(o)).start()

    def wait_wave(w, sems):
        for p, (_, _, size) in enumerate(waves[w]):
            wait_bytes(bias_recv.at[size], sems.at[4 * w + p])

    pl.semaphore_wait(barrier, n - 1)
    start_wave(0)
    assemble(0)
    send_group(send_in, recv_in, ss_in, rs_in, 0)

    def rest(g, _):
        assemble(g)
        return 0

    lax.fori_loop(1, groups, rest, 0)
    wq_t[...] = w_qkv[:, 0:CH].astype(F32).T.astype(BF16)
    wk = w_qkv[:, CH : 2 * CH].astype(F32)
    swapped = pltpu.roll(wk, 2 * HDIM, 1)
    left = lax.broadcasted_iota(jnp.int32, (CH, CH), 1) < 2 * HDIM
    wk_twice[0] = jnp.where(left, wk, swapped).astype(BF16)
    wk_twice[1] = jnp.where(left, swapped, wk).astype(BF16)
    wv_t[...] = w_qkv[:, 2 * CH :].astype(F32).T.astype(BF16)
    queries[...] = jnp.zeros(queries.shape, BF16)
    wait_wave(0, rs_bias)
    start_wave(1)
    wait_wave(1, rs_bias)
    start_wave(2)

    def send_rest(g, _):
        send_group(send_in, recv_in, ss_in, rs_in, g)
        return 0

    def spread_bias(p, _):
        top = upper_half((8, full))
        turn = lambda tile: pltpu.roll(tile, 4, 0)
        px, py = p // 4, lax.rem(p, 4)
        even = bias_recv[px, py, 0].astype(F32) * LOG2E
        odd = bias_recv[px, py, 1].astype(F32) * LOG2E
        for h in range(HEADS):
            tail = slice(64 + h // 2 * 8, 72 + h // 2 * 8)
            even_tail, odd_tail = even[tail], odd[tail]
            if h % 2:
                even_tail = turn(even_tail)
            else:
                odd_tail = turn(odd_tail)
            low, high = turn(odd[16 * h : 16 * h + 8]), turn(odd[16 * h + 8 : 16 * h + 16])
            tiles = [
                even[16 * h : 16 * h + 8], even[16 * h + 8 : 16 * h + 16], jnp.where(top, even_tail, low),
                jnp.where(top, low, high), jnp.where(top, high, odd_tail),
            ]
            for k, tile in enumerate(tiles):
                start = pl.multiple_of(2 * rows * p + 8 * k, 8)
                for i in range(lanes):
                    bias_all[h // 2 * lanes + i, pl.ds(start, 8), h % 2 * CH : (h % 2 + 1) * CH] = tile[
                        :, i * CH : (i + 1) * CH
                    ]
        return 0

    def prepare(g):
        wait_bytes(recv_in.at[g], rs_in.at[g])

        def norm_block(s, _):
            here = pl.ds(pl.multiple_of(8 * block * s, 8 * block), 8 * block)
            normed[here, :] = normalize(recv_in[g, here, :].astype(F32), gain[...], shift[...])
            return 0

        lax.fori_loop(0, n // 8, norm_block, 0)

        def column(b):
            normal = normed[pl.ds(b, full, stride=4), :].astype(BF16)
            query = lax.dot_general(wq_t[...], normal, NT, preferred_element_type=F32)
            query = (query * HDIM ** (-0.5)).astype(BF16).astype(F32) * LOG2E
            high = query.astype(BF16)
            low = (query - high.astype(F32)).astype(BF16)
            for h in range(HEADS):
                own = slice(h * HDIM, (h + 1) * HDIM)
                for i in range(lanes):
                    unit, side, here = (b * 2 + h // 2) * lanes + i, h % 2 * CH, slice(i * CH, (i + 1) * CH)
                    row = h % 2 * HDIM
                    queries[unit, row : row + HDIM, side : side + CH] = high[own, here]
                    queries[unit, 2 * HDIM + row : 3 * HDIM + row, side : side + CH] = low[own, here]
            for p in range(2):
                keys[b, p] = jnp.dot(normal, wk_twice[p], preferred_element_type=F32).astype(BF16)
            v_t[b] = lax.dot_general(wv_t[...], normal, NT, preferred_element_type=F32).astype(BF16)
            gates[b] = jax.nn.sigmoid(jnp.dot(normal, wgate[...], preferred_element_type=F32) + gate_shift[...])

        def columns(b2, _):
            column(2 * b2)
            column(2 * b2 + 1)
            return 0

        lax.fori_loop(0, 2, columns, 0)

    plan = interleave(
        [(3, *c) for c in pieces(full, 128)], [(2, *c) for c in pieces(full, 128)], [(1, *c) for c in pieces(full, 320)]
    )

    def query_block(turn):
        return lax.rem(turn + me, lanes)

    def attend(g):
        def unit(t, slot):
            t1, t3 = jnp.minimum(t, units - 1), jnp.clip(t - 2, 0, units - 1)
            column1, heads1 = lax.rem(t1, 8) // 2, lax.rem(t1, 2)
            place1 = heads1 * lanes + query_block(t1 // 8)
            column3, lane3 = lax.rem(t3, 8) // 2, query_block(t3 // 8)
            heads3 = pl.multiple_of(lax.rem(t3, 2) * 2 * HDIM, 2 * HDIM)
            query = queries[column1 * 2 * lanes + place1]
            top = jnp.max(stats[1 - slot, 0:8, :], axis=0, keepdims=True)
            share = 1.0 / jnp.sum(stats[slot, 8:16, :], axis=0, keepdims=True)
            most = jnp.full((8, 2 * CH), -jnp.inf, F32)
            total = jnp.zeros((8, 2 * CH), F32)
            result = jnp.zeros((2 * HDIM, 2 * CH), F32)
            for step, r, size in plan:
                here = slice(r, r + size)
                if step == 1:
                    score = jnp.dot(keys[column1, heads1, here, :], query, preferred_element_type=F32) + bias_all[place1, here, :]
                    scores[slot, here, :] = score
                    most = jnp.maximum(most, jnp.max(score.reshape(size // 8, 8, 2 * CH), axis=0))
                elif step == 2:
                    power = jnp.exp2(scores[1 - slot, here, :] - top)
                    raised[1 - slot, here, :] = power
                    total = total + jnp.sum(power.reshape(size // 8, 8, 2 * CH), axis=0)
                else:
                    weights = (raised[slot, here, :] * share).astype(BF16)
                    result = result + jnp.dot(
                        v_t[column3, pl.ds(heads3, 2 * HDIM), here], weights, preferred_element_type=F32
                    )
            stats[slot, 0:8, :] = most
            stats[1 - slot, 8:16, :] = total
            attended[column3, lane3, pl.ds(heads3, HDIM), :] = result[0:HDIM, 0:CH]
            attended[column3, lane3, pl.ds(heads3 + HDIM, HDIM), :] = result[HDIM : 2 * HDIM, CH : 2 * CH]

        def two(u, _):
            unit(2 * u, 0)
            unit(2 * u + 1, 1)
            return 0

        def turn(i, _):
            two(4 * i, 0)

            @pl.when(i > 0)
            def _():
                conclude(g, i - 1)

            @pl.when(i < lanes)
            def _():
                lax.fori_loop(4 * i + 1, 4 * i + 4, two, 0)

            return 0

        lax.fori_loop(0, lanes + 1, turn, 0)

    def conclude(g, turn):
        i = query_block(turn)

        for b in range(4):
            rounded = attended[b, i].T.astype(BF16).astype(F32)
            gated = (gates[b, pl.ds(pl.multiple_of(i * CH, CH), CH), :] * rounded).astype(BF16)
            update[pl.ds(b, CH, stride=4), :] = jnp.dot(gated, wout[...], preferred_element_type=F32) + out_shift[...]
        here = pl.ds(pl.multiple_of(4 * CH * i, 4 * CH), 4 * CH)
        send_out[g, here, :] = (update[...] + recv_in[g, here, :].astype(F32)).astype(BF16)

        def give(j, _):
            s = j + jnp.where(j >= me, 1, 0)
            remote(send_out.at[g, chunk(s)], recv_out.at[g, chunk(me)], ss_out.at[g], rs_out.at[g], s).start()
            return 0

        least = (CH * i + rows - 1) // rows - jnp.where((turn > 0) & (i > 0), 1, 0)
        most = CH * (i + 1) // rows + jnp.where((turn == lanes - 1) & (i < lanes - 1), 1, 0)
        lax.fori_loop(least - jnp.where(least > me, 1, 0), most - jnp.where(most > me, 1, 0), give, 0)

        @pl.when((least <= me) & (me < most))
        def _():
            pltpu.make_async_copy(send_out.at[g, chunk(me)], recv_out.at[g, chunk(me)], rs_out.at[g]).start()

    wait_wave(2, rs_bias)
    start_wave(3)
    prepare(0)
    wait_wave(3, rs_bias)
    lax.fori_loop(1, groups, send_rest, 0)
    lax.fori_loop(0, n // 2, spread_bias, 0)

    def group(g, _):
        attend(g)

        @pl.when(g < groups - 1)
        def _():
            prepare(g + 1)

        return 0

    lax.fori_loop(0, groups, group, 0)

    for w in range(4):
        wait_wave(w, ss_bias)

    def drain(g, _):
        wait_bytes(recv_out.at[g], rs_out.at[g])
        wait_bytes(send_in.at[g, pl.ds(0, (n - 1) * block)], ss_in.at[g])
        wait_bytes(send_out.at[g, pl.ds(0, (n - 1) * block)], ss_out.at[g])
        return 0

    lax.fori_loop(0, groups, drain, 0)


def collect(received, out, mix):
    rows, wide, _ = out.shape
    top = upper_half((wide // 8, 8, CH))
    mix[...] = received[0].astype(F32).reshape(mix.shape)
    for a in range(0, rows, 2):
        low = mix[:, 0, 4 * a : 4 * a + 8, :]
        high = mix[:, 1, 4 * a : 4 * a + 8, :]
        out[a] = jnp.where(top, low, pltpu.roll(high, 4, 1)).reshape(wide, CH).astype(BF16)
        out[a + 1] = jnp.where(top, pltpu.roll(low, 4, 1), high).reshape(wide, CH).astype(BF16)


def on_device(n, pair_act, ln_gain, ln_shift, w_qkv, w_bias, w_gate, gate_shift, w_out, out_shift):
    rows, full, channels = pair_act.shape
    groups = full // (4 * n)
    block = 4 * rows
    lanes = full // CH
    vmem = pl.BlockSpec(memory_space=pltpu.VMEM)
    dma = pltpu.SemaphoreType.DMA
    received = pl.pallas_call(
        functools.partial(kernel, n),
        out_shape=jax.ShapeDtypeStruct((groups, n * block, CH), BF16),
        in_specs=[vmem] * 9,
        out_specs=pl.BlockSpec(memory_space=pl.ANY),
        scratch_shapes=[
            pltpu.VMEM((groups, n * block, CH), BF16),
            pltpu.VMEM((groups, n * block, CH), BF16),
            pltpu.VMEM((groups, n * block, CH), BF16),
            pltpu.VMEM((4, 4, 2, HEADS * rows, full), BF16),
            pltpu.VMEM((2 * lanes, full, 2 * CH), F32),
            pltpu.VMEM((n // 2, 2, block, CH), F32),
            pltpu.VMEM((n * block, CH), F32),
            pltpu.VMEM((4 * CH, CH), F32),
            pltpu.VMEM((HEADS * rows, full), F32),
            pltpu.VMEM((CH, CH), BF16),
            pltpu.VMEM((2, CH, CH), BF16),
            pltpu.VMEM((CH, CH), BF16),
            pltpu.VMEM((8 * lanes, CH, 2 * CH), BF16),
            pltpu.VMEM((4, 2, full, CH), BF16),
            pltpu.VMEM((4, CH, full), BF16),
            pltpu.VMEM((4, full, CH), F32),
            pltpu.VMEM((2, full, 2 * CH), F32),
            pltpu.VMEM((2, full, 2 * CH), F32),
            pltpu.VMEM((2, 16, 2 * CH), F32),
            pltpu.VMEM((4, lanes, CH, CH), F32),
            dma((16,)), dma((16,)), dma((groups,)), dma((groups,)), dma((groups,)), dma((groups,)),
        ],
        compiler_params=pltpu.CompilerParams(
            collective_id=0, has_side_effects=True, vmem_limit_bytes=56 * 2**20
        ),
        name="triangle",
    )(
        pair_act, ln_gain[None], ln_shift[None], w_qkv, w_bias.T, w_gate, gate_shift[None], w_out, out_shift[None],
    )
    return pl.pallas_call(
        collect,
        grid=(groups,),
        out_shape=jax.ShapeDtypeStruct(pair_act.shape, BF16),
        in_specs=[pl.BlockSpec((1, n * block, CH), lambda g: (g, 0, 0))],
        out_specs=pl.BlockSpec((rows, 4 * n, CH), lambda g: (0, g, 0)),
        scratch_shapes=[pltpu.VMEM((n // 2, 2, block, CH), F32)],
        compiler_params=pltpu.CompilerParams(vmem_limit_bytes=60 * 2**20),
        name="collect",
    )(received)


def solution(mesh):
    in_specs = (P(("dp", "axial"), None, None), P(), P(), P(), P(), P(), P(), P(), P())
    out_specs = P(("dp", "axial"), None, None)
    return jax.shard_map(
        functools.partial(on_device, mesh.shape["axial"]),
        mesh=mesh, in_specs=in_specs, out_specs=out_specs, check_vma=False,
    )
```

```python
import functools

import jax
import jax.numpy as jnp
from jax import lax
from jax.experimental import pallas as pl
from jax.experimental.pallas import tpu as pltpu
from jax.sharding import PartitionSpec as P

HEADS = 4
HDIM = 32
CH = 128
LOG2E = 1.4426950408889634
MESH = pl.DeviceIdType.MESH
F32 = jnp.float32
BF16 = jnp.bfloat16
NT = (((1,), (1,)), ((), ()))


def normalize(values, gain, shift):
    center = jnp.mean(values, axis=-1, keepdims=True)
    spread = jnp.mean((values - center) ** 2, axis=-1, keepdims=True)
    return (values - center) * lax.rsqrt(spread + 1e-05) * gain + shift


def upper_half(shape):
    return lax.broadcasted_iota(jnp.int32, shape, len(shape) - 2) < 4


def balanced_offsets():
    rest = [(x, y, z) for x in range(4) for y in range(4) for z in range(2) if x or y or z]

    def load(o):
        out = [0] * 6
        for axis, step in enumerate((o[0], o[1], 2 * o[2])):
            out[2 * axis] += step in (1, 2)
            out[2 * axis + 1] += step in (2, 3)
        return out

    total, order = [0] * 6, []
    while rest:
        def cost(o):
            new = [t + a for t, a in zip(total, load(o))]
            return max(new) * 100 + sum(n * n for n in new), -sum(load(o))
        best = min(rest, key=cost)
        rest.remove(best)
        order.append(best)
        total = [t + a for t, a in zip(total, load(best))]
    return order


OFFSETS = balanced_offsets()


def pieces(full, size):
    return [(r, min(size, full - r)) for r in range(0, full, size)]


def interleave(*plans):
    done, out = [0] * len(plans), []
    for _ in range(sum(map(len, plans))):
        i = min(
            (i for i in range(len(plans)) if done[i] < len(plans[i])),
            key=lambda i: (done[i] + 0.5) / len(plans[i]),
        )
        out.append(plans[i][done[i]])
        done[i] += 1
    return out


def kernel(
    n, pair, gain, shift, w_qkv, w_bias, wgate, gate_shift, wout, out_shift, recv_out,
    send_in, recv_in, send_out, bias_recv, bias_all,
    mix, normed, update, rows_bias, wq_t, wk_twice, wv_t, queries, keys, v_t, gates, scores, raised, stats, attended,
    ss_bias, rs_bias, ss_in, rs_in, ss_out, rs_out,
):
    rows, full, _ = pair.shape
    groups = send_in.shape[0]
    block = 4 * rows
    wide = n * 4
    lanes = full // CH
    units = 4 * 2 * lanes
    me = lax.axis_index("axial")
    x, y, z = me // 8, lax.rem(me // 2, 4), lax.rem(me, 2)

    def peer(o):
        return (lax.rem(x + o[0], 4) * 4 + lax.rem(y + o[1], 4)) * 2 + lax.rem(z + o[2], 2)

    barrier = pltpu.get_barrier_semaphore()
    for o in OFFSETS:
        pl.semaphore_signal(barrier, inc=1, device_id={"axial": peer(o)}, device_id_type=MESH)

    def remote(src, dst, ss, rs, to):
        return pltpu.make_async_remote_copy(
            src_ref=src, dst_ref=dst, send_sem=ss, recv_sem=rs, device_id={"axial": to}, device_id_type=MESH
        )

    def chunk(d):
        return pl.ds(pl.multiple_of(d * block, block), block)

    def wait_bytes(ref, sem):
        pltpu.make_async_copy(ref, ref, sem).wait()

    def assemble(g):
        top = upper_half((n // 2, 8, CH))
        here = pl.ds(pl.multiple_of(g * wide, wide), wide)
        for a in range(0, rows, 2):
            even = pair[a, here, :].astype(F32).reshape(n // 2, 8, CH)
            odd = pair[a + 1, here, :].astype(F32).reshape(n // 2, 8, CH)
            mix[:, 0, 4 * a : 4 * a + 8, :] = jnp.where(top, even, pltpu.roll(odd, 4, 1))
            mix[:, 1, 4 * a : 4 * a + 8, :] = jnp.where(top, pltpu.roll(even, 4, 1), odd)
        send_in[g] = mix[...].astype(BF16).reshape(n * block, CH)

    def send_group(src, dst, ss, rs, g):
        for o in OFFSETS:
            to = peer(o)
            remote(src.at[g, chunk(to)], dst.at[g, chunk(me)], ss.at[g], rs.at[g], to).start()
        pltpu.make_async_copy(src.at[g, chunk(me)], dst.at[g, chunk(me)], rs.at[g]).start()

    wbias_t = w_bias[...]

    def bias_rows(k4, _):
        for k in range(4):
            normal = normalize(pair[4 * k4 + k].astype(F32), gain[...], shift[...]).astype(BF16)
            line = lax.dot_general(wbias_t, normal, NT, preferred_element_type=F32)
            for h in range(HEADS):
                place = jnp.where(k4 < 4, h * 16 + 4 * k4, 4 * h + 64) + k
                rows_bias[pl.ds(place, 1), :] = line[h : h + 1, :]
        return 0

    lax.fori_loop(0, rows // 4, bias_rows, 0)
    bias_recv[x, y, z] = rows_bias[...].astype(BF16)

    first, second, third = slice(0, 32), slice(32, 64), slice(64, 80)
    every = slice(None)
    three = slice(0, 3)
    lower, upper = slice(0, 2), slice(2, 4)
    before = lambda place: lax.rem(place + 3, 4)
    after = lambda place: lax.rem(place + 1, 4)
    to_x = [(1, 0, 0), (3, 0, 0), (2, 0, 0)]
    to_y = [(0, 1, 0), (0, 3, 0), (0, 2, 0)]
    to_z = [(0, 0, 1)]
    waves = [
        [((x, y, z, first), to_z, (0, 0, 0, first)), ((x, y, z, second), to_x, (three, 0, 0, second)),
         ((x, y, z, third), to_y, (0, three, 0, third))],
        [((x, y, every, first), to_y, (0, three, every, first)), ((every, y, z, second), to_z, (every, 0, 0, second)),
         ((x, every, z, third), to_x, (three, every, 0, third))],
        [((x, every, every, first), to_x[:2], (lower, every, every, first)),
         ((every, y, every, second), to_y[:2], (every, lower, every, second)),
         ((every, every, z, third), to_z, (every, every, 0, third))],
        [((before(x), lower, every, first), to_x[:1], (0, lower, every, first)),
         ((after(x), upper, every, first), to_x[1:2], (0, lower, every, first)),
         ((lower, before(y), every, second), to_y[:1], (lower, 0, every, second)),
         ((upper, after(y), every, second), to_y[1:2], (lower, 0, every, second))],
    ]

    def start_wave(w):
        for p, (part, targets, _) in enumerate(waves[w]):
            for o in targets:
                remote(bias_recv.at[part], bias_recv.at[part], ss_bias.at[4 * w + p], rs_bias.at[4 * w + p], peer(o)).start()

    def wait_wave(w, sems):
        for p, (_, _, size) in enumerate(waves[w]):
            wait_bytes(bias_recv.at[size], sems.at[4 * w + p])

    pl.semaphore_wait(barrier, n - 1)
    start_wave(0)
    assemble(0)

    def rest(g, _):
        assemble(g)
        return 0

    lax.fori_loop(1, groups, rest, 0)
    wq_t[...] = w_qkv[:, 0:CH].astype(F32).T.astype(BF16)
    wk = w_qkv[:, CH : 2 * CH].astype(F32)
    swapped = pltpu.roll(wk, 2 * HDIM, 1)
    left = lax.broadcasted_iota(jnp.int32, (CH, CH), 1) < 2 * HDIM
    wk_twice[0] = jnp.where(left, wk, swapped).astype(BF16)
    wk_twice[1] = jnp.where(left, swapped, wk).astype(BF16)
    wv_t[...] = w_qkv[:, 2 * CH :].astype(F32).T.astype(BF16)
    queries[...] = jnp.zeros(queries.shape, BF16)
    wait_wave(0, rs_bias)
    start_wave(1)
    send_group(send_in, recv_in, ss_in, rs_in, 0)
    wait_wave(1, rs_bias)
    start_wave(2)

    def send_rest(g, _):
        send_group(send_in, recv_in, ss_in, rs_in, g)
        return 0

    def spread_bias(p, _):
        top = upper_half((8, full))
        turn = lambda tile: pltpu.roll(tile, 4, 0)
        px, py = p // 4, lax.rem(p, 4)
        even = bias_recv[px, py, 0].astype(F32) * LOG2E
        odd = bias_recv[px, py, 1].astype(F32) * LOG2E
        for h in range(HEADS):
            tail = slice(64 + h // 2 * 8, 72 + h // 2 * 8)
            even_tail, odd_tail = even[tail], odd[tail]
            if h % 2:
                even_tail = turn(even_tail)
            else:
                odd_tail = turn(odd_tail)
            low, high = turn(odd[16 * h : 16 * h + 8]), turn(odd[16 * h + 8 : 16 * h + 16])
            tiles = [
                even[16 * h : 16 * h + 8], even[16 * h + 8 : 16 * h + 16], jnp.where(top, even_tail, low),
                jnp.where(top, low, high), jnp.where(top, high, odd_tail),
            ]
            for k, tile in enumerate(tiles):
                start = pl.multiple_of(2 * rows * p + 8 * k, 8)
                for i in range(lanes):
                    bias_all[h // 2 * lanes + i, pl.ds(start, 8), h % 2 * CH : (h % 2 + 1) * CH] = tile[
                        :, i * CH : (i + 1) * CH
                    ]
        return 0

    def prepare(g):
        wait_bytes(recv_in.at[g], rs_in.at[g])

        def norm_block(s, _):
            here = pl.ds(pl.multiple_of(8 * block * s, 8 * block), 8 * block)
            normed[here, :] = normalize(recv_in[g, here, :].astype(F32), gain[...], shift[...])
            return 0

        lax.fori_loop(0, n // 8, norm_block, 0)

        def column(b):
            normal = normed[pl.ds(b, full, stride=4), :].astype(BF16)
            query = lax.dot_general(wq_t[...], normal, NT, preferred_element_type=F32)
            query = (query * HDIM ** (-0.5)).astype(BF16).astype(F32) * LOG2E
            high = query.astype(BF16)
            low = (query - high.astype(F32)).astype(BF16)
            for h in range(HEADS):
                own = slice(h * HDIM, (h + 1) * HDIM)
                for i in range(lanes):
                    unit, side, here = (b * 2 + h // 2) * lanes + i, h % 2 * CH, slice(i * CH, (i + 1) * CH)
                    row = h % 2 * HDIM
                    queries[unit, row : row + HDIM, side : side + CH] = high[own, here]
                    queries[unit, 2 * HDIM + row : 3 * HDIM + row, side : side + CH] = low[own, here]
            for p in range(2):
                keys[b, p] = jnp.dot(normal, wk_twice[p], preferred_element_type=F32).astype(BF16)
            v_t[b] = lax.dot_general(wv_t[...], normal, NT, preferred_element_type=F32).astype(BF16)
            gates[b] = jax.nn.sigmoid(jnp.dot(normal, wgate[...], preferred_element_type=F32) + gate_shift[...])

        def columns(b2, _):
            column(2 * b2)
            column(2 * b2 + 1)
            return 0

        lax.fori_loop(0, 2, columns, 0)

    plan = interleave(
        [(1, *c) for c in pieces(full, 320)], [(2, *c) for c in pieces(full, 128)], [(3, *c) for c in pieces(full, 256)]
    )

    def query_block(turn):
        return lax.rem(turn + me, lanes)

    def attend(g):
        def unit(t, slot):
            t1, t3 = jnp.minimum(t, units - 1), jnp.clip(t - 2, 0, units - 1)
            column1, heads1 = lax.rem(t1, 8) // 2, lax.rem(t1, 2)
            place1 = heads1 * lanes + query_block(t1 // 8)
            column3, lane3 = lax.rem(t3, 8) // 2, query_block(t3 // 8)
            heads3 = pl.multiple_of(lax.rem(t3, 2) * 2 * HDIM, 2 * HDIM)
            query = queries[column1 * 2 * lanes + place1]
            top = jnp.max(stats[1 - slot, 0:8, :], axis=0, keepdims=True)
            share = 1.0 / jnp.sum(stats[slot, 8:16, :], axis=0, keepdims=True)
            most = jnp.full((8, 2 * CH), -jnp.inf, F32)
            total = jnp.zeros((8, 2 * CH), F32)
            result = jnp.zeros((2 * HDIM, 2 * CH), F32)
            for step, r, size in plan:
                here = slice(r, r + size)
                if step == 1:
                    score = jnp.dot(keys[column1, heads1, here, :], query, preferred_element_type=F32) + bias_all[place1, here, :]
                    scores[slot, here, :] = score
                    most = jnp.maximum(most, jnp.max(score.reshape(size // 8, 8, 2 * CH), axis=0))
                elif step == 2:
                    power = jnp.exp2(scores[1 - slot, here, :] - top)
                    raised[1 - slot, here, :] = power
                    total = total + jnp.sum(power.reshape(size // 8, 8, 2 * CH), axis=0)
                else:
                    weights = (raised[slot, here, :] * share).astype(BF16)
                    result = result + jnp.dot(
                        v_t[column3, pl.ds(heads3, 2 * HDIM), here], weights, preferred_element_type=F32
                    )
            stats[slot, 0:8, :] = most
            stats[1 - slot, 8:16, :] = total
            attended[column3, lane3, pl.ds(heads3, HDIM), :] = result[0:HDIM, 0:CH]
            attended[column3, lane3, pl.ds(heads3 + HDIM, HDIM), :] = result[HDIM : 2 * HDIM, CH : 2 * CH]

        def two(u, _):
            unit(2 * u, 0)
            unit(2 * u + 1, 1)
            return 0

        def turn(i, _):
            two(4 * i, 0)

            @pl.when(i > 0)
            def _():
                conclude(g, i - 1)

            @pl.when(i < lanes)
            def _():
                lax.fori_loop(4 * i + 1, 4 * i + 4, two, 0)

            return 0

        lax.fori_loop(0, lanes + 1, turn, 0)

    def conclude(g, turn):
        i = query_block(turn)

        for b in range(4):
            rounded = attended[b, i].T.astype(BF16).astype(F32)
            gated = (gates[b, pl.ds(pl.multiple_of(i * CH, CH), CH), :] * rounded).astype(BF16)
            update[pl.ds(b, CH, stride=4), :] = jnp.dot(gated, wout[...], preferred_element_type=F32) + out_shift[...]
        here = pl.ds(pl.multiple_of(4 * CH * i, 4 * CH), 4 * CH)
        send_out[g, here, :] = (update[...] + recv_in[g, here, :].astype(F32)).astype(BF16)

        def give(j, _):
            s = j + jnp.where(j >= me, 1, 0)
            remote(send_out.at[g, chunk(s)], recv_out.at[g, chunk(me)], ss_out.at[g], rs_out.at[g], s).start()
            return 0

        least = (CH * i + rows - 1) // rows - jnp.where((turn > 0) & (i > 0), 1, 0)
        most = CH * (i + 1) // rows + jnp.where((turn == lanes - 1) & (i < lanes - 1), 1, 0)
        lax.fori_loop(least - jnp.where(least > me, 1, 0), most - jnp.where(most > me, 1, 0), give, 0)

        @pl.when((least <= me) & (me < most))
        def _():
            pltpu.make_async_copy(send_out.at[g, chunk(me)], recv_out.at[g, chunk(me)], rs_out.at[g]).start()

    wait_wave(2, rs_bias)
    start_wave(3)
    prepare(0)
    wait_wave(3, rs_bias)
    lax.fori_loop(1, groups, send_rest, 0)
    lax.fori_loop(0, n // 2, spread_bias, 0)

    def group(g, _):
        attend(g)

        @pl.when(g < groups - 1)
        def _():
            prepare(g + 1)

        return 0

    lax.fori_loop(0, groups, group, 0)

    for w in range(4):
        wait_wave(w, ss_bias)

    def drain(g, _):
        wait_bytes(recv_out.at[g], rs_out.at[g])
        wait_bytes(send_in.at[g, pl.ds(0, (n - 1) * block)], ss_in.at[g])
        wait_bytes(send_out.at[g, pl.ds(0, (n - 1) * block)], ss_out.at[g])
        return 0

    lax.fori_loop(0, groups, drain, 0)


def collect(received, out, mix):
    rows, wide, _ = out.shape
    top = upper_half((wide // 8, 8, CH))
    mix[...] = received[0].astype(F32).reshape(mix.shape)
    for a in range(0, rows, 2):
        low = mix[:, 0, 4 * a : 4 * a + 8, :]
        high = mix[:, 1, 4 * a : 4 * a + 8, :]
        out[a] = jnp.where(top, low, pltpu.roll(high, 4, 1)).reshape(wide, CH).astype(BF16)
        out[a + 1] = jnp.where(top, pltpu.roll(low, 4, 1), high).reshape(wide, CH).astype(BF16)


def on_device(n, pair_act, ln_gain, ln_shift, w_qkv, w_bias, w_gate, gate_shift, w_out, out_shift):
    rows, full, channels = pair_act.shape
    groups = full // (4 * n)
    block = 4 * rows
    lanes = full // CH
    vmem = pl.BlockSpec(memory_space=pltpu.VMEM)
    dma = pltpu.SemaphoreType.DMA
    received = pl.pallas_call(
        functools.partial(kernel, n),
        out_shape=jax.ShapeDtypeStruct((groups, n * block, CH), BF16),
        in_specs=[vmem] * 9,
        out_specs=pl.BlockSpec(memory_space=pl.ANY),
        scratch_shapes=[
            pltpu.VMEM((groups, n * block, CH), BF16),
            pltpu.VMEM((groups, n * block, CH), BF16),
            pltpu.VMEM((groups, n * block, CH), BF16),
            pltpu.VMEM((4, 4, 2, HEADS * rows, full), BF16),
            pltpu.VMEM((2 * lanes, full, 2 * CH), F32),
            pltpu.VMEM((n // 2, 2, block, CH), F32),
            pltpu.VMEM((n * block, CH), F32),
            pltpu.VMEM((4 * CH, CH), F32),
            pltpu.VMEM((HEADS * rows, full), F32),
            pltpu.VMEM((CH, CH), BF16),
            pltpu.VMEM((2, CH, CH), BF16),
            pltpu.VMEM((CH, CH), BF16),
            pltpu.VMEM((8 * lanes, CH, 2 * CH), BF16),
            pltpu.VMEM((4, 2, full, CH), BF16),
            pltpu.VMEM((4, CH, full), BF16),
            pltpu.VMEM((4, full, CH), F32),
            pltpu.VMEM((2, full, 2 * CH), F32),
            pltpu.VMEM((2, full, 2 * CH), F32),
            pltpu.VMEM((2, 16, 2 * CH), F32),
            pltpu.VMEM((4, lanes, CH, CH), F32),
            dma((16,)), dma((16,)), dma((groups,)), dma((groups,)), dma((groups,)), dma((groups,)),
        ],
        compiler_params=pltpu.CompilerParams(
            collective_id=0, has_side_effects=True, vmem_limit_bytes=56 * 2**20
        ),
        name="triangle",
    )(
        pair_act, ln_gain[None], ln_shift[None], w_qkv, w_bias.T, w_gate, gate_shift[None], w_out, out_shift[None],
    )
    return pl.pallas_call(
        collect,
        grid=(groups,),
        out_shape=jax.ShapeDtypeStruct(pair_act.shape, BF16),
        in_specs=[pl.BlockSpec((1, n * block, CH), lambda g: (g, 0, 0))],
        out_specs=pl.BlockSpec((rows, 4 * n, CH), lambda g: (0, g, 0)),
        scratch_shapes=[pltpu.VMEM((n // 2, 2, block, CH), F32)],
        compiler_params=pltpu.CompilerParams(vmem_limit_bytes=60 * 2**20),
        name="collect",
    )(received)


def solution(mesh):
    in_specs = (P(("dp", "axial"), None, None), P(), P(), P(), P(), P(), P(), P(), P())
    out_specs = P(("dp", "axial"), None, None)
    return jax.shard_map(
        functools.partial(on_device, mesh.shape["axial"]),
        mesh=mesh, in_specs=in_specs, out_specs=out_specs, check_vma=False,
    )
```

```python
import functools

import jax
import jax.numpy as jnp
from jax import lax
from jax.experimental import pallas as pl
from jax.experimental.pallas import tpu as pltpu
from jax.sharding import PartitionSpec as P

HEADS = 4
HDIM = 32
CH = 128
LOG2E = 1.4426950408889634
MESH = pl.DeviceIdType.MESH
F32 = jnp.float32
BF16 = jnp.bfloat16
NT = (((1,), (1,)), ((), ()))


def normalize(values, gain, shift):
    center = jnp.mean(values, axis=-1, keepdims=True)
    spread = jnp.mean((values - center) ** 2, axis=-1, keepdims=True)
    return (values - center) * lax.rsqrt(spread + 1e-05) * gain + shift


def upper_half(shape):
    return lax.broadcasted_iota(jnp.int32, shape, len(shape) - 2) < 4


def balanced_offsets():
    rest = [(x, y, z) for x in range(4) for y in range(4) for z in range(2) if x or y or z]

    def load(o):
        out = [0] * 6
        for axis, step in enumerate((o[0], o[1], 2 * o[2])):
            out[2 * axis] += step in (1, 2)
            out[2 * axis + 1] += step in (2, 3)
        return out

    total, order = [0] * 6, []
    while rest:
        def cost(o):
            new = [t + a for t, a in zip(total, load(o))]
            return max(new) * 100 + sum(n * n for n in new), -sum(load(o))
        best = min(rest, key=cost)
        rest.remove(best)
        order.append(best)
        total = [t + a for t, a in zip(total, load(best))]
    return order


OFFSETS = balanced_offsets()


def pieces(full, size):
    return [(r, min(size, full - r)) for r in range(0, full, size)]


def interleave(*plans):
    done, out = [0] * len(plans), []
    for _ in range(sum(map(len, plans))):
        i = min(
            (i for i in range(len(plans)) if done[i] < len(plans[i])),
            key=lambda i: (done[i] + 0.5) / len(plans[i]),
        )
        out.append(plans[i][done[i]])
        done[i] += 1
    return out


def kernel(
    n, pair, gain, shift, w_qkv, w_bias, wgate, gate_shift, wout, out_shift, recv_out,
    send_in, recv_in, send_out, bias_recv, bias_all,
    mix, normed, update, rows_bias, wq_t, wk_twice, wv_t, queries, keys, v_t, gates, scores, raised, stats, attended,
    ss_bias, rs_bias, ss_in, rs_in, ss_out, rs_out,
):
    rows, full, _ = pair.shape
    groups = send_in.shape[0]
    block = 4 * rows
    wide = n * 4
    lanes = full // CH
    units = 4 * 2 * lanes
    me = lax.axis_index("axial")
    x, y, z = me // 8, lax.rem(me // 2, 4), lax.rem(me, 2)

    def peer(o):
        return (lax.rem(x + o[0], 4) * 4 + lax.rem(y + o[1], 4)) * 2 + lax.rem(z + o[2], 2)

    barrier = pltpu.get_barrier_semaphore()
    for o in OFFSETS:
        pl.semaphore_signal(barrier, inc=1, device_id={"axial": peer(o)}, device_id_type=MESH)

    def remote(src, dst, ss, rs, to):
        return pltpu.make_async_remote_copy(
            src_ref=src, dst_ref=dst, send_sem=ss, recv_sem=rs, device_id={"axial": to}, device_id_type=MESH
        )

    def chunk(d):
        return pl.ds(pl.multiple_of(d * block, block), block)

    def wait_bytes(ref, sem):
        pltpu.make_async_copy(ref, ref, sem).wait()

    def assemble(g):
        top = upper_half((n // 2, 8, CH))
        here = pl.ds(pl.multiple_of(g * wide, wide), wide)
        for a in range(0, rows, 2):
            even = pair[a, here, :].astype(F32).reshape(n // 2, 8, CH)
            odd = pair[a + 1, here, :].astype(F32).reshape(n // 2, 8, CH)
            mix[:, 0, 4 * a : 4 * a + 8, :] = jnp.where(top, even, pltpu.roll(odd, 4, 1))
            mix[:, 1, 4 * a : 4 * a + 8, :] = jnp.where(top, pltpu.roll(even, 4, 1), odd)
        send_in[g] = mix[...].astype(BF16).reshape(n * block, CH)

    def send_group(src, dst, ss, rs, g):
        for o in OFFSETS:
            to = peer(o)
            remote(src.at[g, chunk(to)], dst.at[g, chunk(me)], ss.at[g], rs.at[g], to).start()
        pltpu.make_async_copy(src.at[g, chunk(me)], dst.at[g, chunk(me)], rs.at[g]).start()

    wbias_t = w_bias[...]

    def bias_rows(k4, _):
        for k in range(4):
            normal = normalize(pair[4 * k4 + k].astype(F32), gain[...], shift[...]).astype(BF16)
            line = lax.dot_general(wbias_t, normal, NT, preferred_element_type=F32)
            for h in range(HEADS):
                place = jnp.where(k4 < 4, h * 16 + 4 * k4, 4 * h + 64) + k
                rows_bias[pl.ds(place, 1), :] = line[h : h + 1, :]
        return 0

    lax.fori_loop(0, rows // 4, bias_rows, 0)
    bias_recv[x, y, z] = rows_bias[...].astype(BF16)

    first, second, third = slice(0, 32), slice(32, 64), slice(64, 80)
    every = slice(None)
    three = slice(0, 3)
    lower, upper = slice(0, 2), slice(2, 4)
    before = lambda place: lax.rem(place + 3, 4)
    after = lambda place: lax.rem(place + 1, 4)
    to_x = [(1, 0, 0), (3, 0, 0), (2, 0, 0)]
    to_y = [(0, 1, 0), (0, 3, 0), (0, 2, 0)]
    to_z = [(0, 0, 1)]
    waves = [
        [((x, y, z, first), to_z, (0, 0, 0, first)), ((x, y, z, second), to_x, (three, 0, 0, second)),
         ((x, y, z, third), to_y, (0, three, 0, third))],
        [((x, y, every, first), to_y, (0, three, every, first)), ((every, y, z, second), to_z, (every, 0, 0, second)),
         ((x, every, z, third), to_x, (three, every, 0, third))],
        [((x, every, every, first), to_x[:2], (lower, every, every, first)),
         ((every, y, every, second), to_y[:2], (every, lower, every, second)),
         ((every, every, z, third), to_z, (every, every, 0, third))],
        [((before(x), lower, every, first), to_x[:1], (0, lower, every, first)),
         ((after(x), upper, every, first), to_x[1:2], (0, lower, every, first)),
         ((lower, before(y), every, second), to_y[:1], (lower, 0, every, second)),
         ((upper, after(y), every, second), to_y[1:2], (lower, 0, every, second))],
    ]

    def start_wave(w):
        for p, (part, targets, _) in enumerate(waves[w]):
            for o in targets:
                remote(bias_recv.at[part], bias_recv.at[part], ss_bias.at[4 * w + p], rs_bias.at[4 * w + p], peer(o)).start()

    def wait_wave(w, sems):
        for p, (_, _, size) in enumerate(waves[w]):
            wait_bytes(bias_recv.at[size], sems.at[4 * w + p])

    pl.semaphore_wait(barrier, n - 1)
    start_wave(0)
    assemble(0)

    def rest(g, _):
        assemble(g)
        return 0

    lax.fori_loop(1, groups, rest, 0)
    wq_t[...] = w_qkv[:, 0:CH].astype(F32).T.astype(BF16)
    wk = w_qkv[:, CH : 2 * CH].astype(F32)
    swapped = pltpu.roll(wk, 2 * HDIM, 1)
    left = lax.broadcasted_iota(jnp.int32, (CH, CH), 1) < 2 * HDIM
    wk_twice[0] = jnp.where(left, wk, swapped).astype(BF16)
    wk_twice[1] = jnp.where(left, swapped, wk).astype(BF16)
    wv_t[...] = w_qkv[:, 2 * CH :].astype(F32).T.astype(BF16)
    queries[...] = jnp.zeros(queries.shape, BF16)
    wait_wave(0, rs_bias)
    start_wave(1)
    send_group(send_in, recv_in, ss_in, rs_in, 0)
    wait_wave(1, rs_bias)
    start_wave(2)

    def send_rest(g, _):
        send_group(send_in, recv_in, ss_in, rs_in, g)
        return 0

    def spread_bias(p, _):
        top = upper_half((8, full))
        turn = lambda tile: pltpu.roll(tile, 4, 0)
        px, py = p // 4, lax.rem(p, 4)
        even = bias_recv[px, py, 0].astype(F32) * LOG2E
        odd = bias_recv[px, py, 1].astype(F32) * LOG2E
        for h in range(HEADS):
            tail = slice(64 + h // 2 * 8, 72 + h // 2 * 8)
            even_tail, odd_tail = even[tail], odd[tail]
            if h % 2:
                even_tail = turn(even_tail)
            else:
                odd_tail = turn(odd_tail)
            low, high = turn(odd[16 * h : 16 * h + 8]), turn(odd[16 * h + 8 : 16 * h + 16])
            tiles = [
                even[16 * h : 16 * h + 8], even[16 * h + 8 : 16 * h + 16], jnp.where(top, even_tail, low),
                jnp.where(top, low, high), jnp.where(top, high, odd_tail),
            ]
            for k, tile in enumerate(tiles):
                start = pl.multiple_of(2 * rows * p + 8 * k, 8)
                for i in range(lanes):
                    bias_all[h // 2 * lanes + i, pl.ds(start, 8), h % 2 * CH : (h % 2 + 1) * CH] = tile[
                        :, i * CH : (i + 1) * CH
                    ]
        return 0

    def prepare(g):
        wait_bytes(recv_in.at[g], rs_in.at[g])

        def norm_block(s, _):
            here = pl.ds(pl.multiple_of(8 * block * s, 8 * block), 8 * block)
            normed[here, :] = normalize(recv_in[g, here, :].astype(F32), gain[...], shift[...])
            return 0

        lax.fori_loop(0, n // 8, norm_block, 0)

        def column(b):
            normal = normed[pl.ds(b, full, stride=4), :].astype(BF16)
            query = lax.dot_general(wq_t[...], normal, NT, preferred_element_type=F32)
            query = (query * HDIM ** (-0.5)).astype(BF16).astype(F32) * LOG2E
            high = query.astype(BF16)
            low = (query - high.astype(F32)).astype(BF16)
            for h in range(HEADS):
                own = slice(h * HDIM, (h + 1) * HDIM)
                for i in range(lanes):
                    unit, side, here = (b * 2 + h // 2) * lanes + i, h % 2 * CH, slice(i * CH, (i + 1) * CH)
                    row = h % 2 * HDIM
                    queries[unit, row : row + HDIM, side : side + CH] = high[own, here]
                    queries[unit, 2 * HDIM + row : 3 * HDIM + row, side : side + CH] = low[own, here]
            for p in range(2):
                keys[b, p] = jnp.dot(normal, wk_twice[p], preferred_element_type=F32).astype(BF16)
            v_t[b] = lax.dot_general(wv_t[...], normal, NT, preferred_element_type=F32).astype(BF16)
            gates[b] = jax.nn.sigmoid(jnp.dot(normal, wgate[...], preferred_element_type=F32) + gate_shift[...])

        def columns(b2, _):
            column(2 * b2)
            column(2 * b2 + 1)
            return 0

        lax.fori_loop(0, 2, columns, 0)

    plan = interleave(
        [(1, *c) for c in pieces(full, 320)], [(2, *c) for c in pieces(full, 128)], [(3, *c) for c in pieces(full, 256)]
    )

    def query_block(turn):
        return lax.rem(turn + me, lanes)

    def attend(g):
        def unit(t, slot):
            t1, t3 = jnp.minimum(t, units - 1), jnp.clip(t - 2, 0, units - 1)
            column1, heads1 = lax.rem(t1, 8) // 2, lax.rem(t1, 2)
            place1 = heads1 * lanes + query_block(t1 // 8)
            column3, lane3 = lax.rem(t3, 8) // 2, query_block(t3 // 8)
            heads3 = pl.multiple_of(lax.rem(t3, 2) * 2 * HDIM, 2 * HDIM)
            query = queries[column1 * 2 * lanes + place1]
            top = jnp.max(stats[1 - slot, 0:8, :], axis=0, keepdims=True)
            share = 1.0 / jnp.sum(stats[slot, 8:16, :], axis=0, keepdims=True)
            most = jnp.full((8, 2 * CH), -jnp.inf, F32)
            total = jnp.zeros((8, 2 * CH), F32)
            result = jnp.zeros((2 * HDIM, 2 * CH), F32)
            for step, r, size in plan:
                here = slice(r, r + size)
                if step == 1:
                    score = jnp.dot(keys[column1, heads1, here, :], query, preferred_element_type=F32) + bias_all[place1, here, :]
                    scores[slot, here, :] = score
                    most = jnp.maximum(most, jnp.max(score.reshape(size // 8, 8, 2 * CH), axis=0))
                elif step == 2:
                    power = jnp.exp2(scores[1 - slot, here, :] - top)
                    raised[1 - slot, here, :] = power
                    total = total + jnp.sum(power.reshape(size // 8, 8, 2 * CH), axis=0)
                else:
                    weights = (raised[slot, here, :] * share).astype(BF16)
                    result = result + jnp.dot(
                        v_t[column3, pl.ds(heads3, 2 * HDIM), here], weights, preferred_element_type=F32
                    )
            stats[slot, 0:8, :] = most
            stats[1 - slot, 8:16, :] = total
            attended[column3, lane3, pl.ds(heads3, HDIM), :] = result[0:HDIM, 0:CH]
            attended[column3, lane3, pl.ds(heads3 + HDIM, HDIM), :] = result[HDIM : 2 * HDIM, CH : 2 * CH]

        def two(u, _):
            unit(2 * u, 0)
            unit(2 * u + 1, 1)
            return 0

        def turn(i, _):
            two(4 * i, 0)

            @pl.when(i > 0)
            def _():
                conclude(g, i - 1)

            @pl.when(i < lanes)
            def _():
                lax.fori_loop(4 * i + 1, 4 * i + 4, two, 0)

            return 0

        lax.fori_loop(0, lanes + 1, turn, 0)

    def conclude(g, turn):
        i = query_block(turn)

        for b in range(4):
            rounded = attended[b, i].T.astype(BF16).astype(F32)
            gated = (gates[b, pl.ds(pl.multiple_of(i * CH, CH), CH), :] * rounded).astype(BF16)
            update[pl.ds(b, CH, stride=4), :] = jnp.dot(gated, wout[...], preferred_element_type=F32) + out_shift[...]
        here = pl.ds(pl.multiple_of(4 * CH * i, 4 * CH), 4 * CH)
        send_out[g, here, :] = (update[...] + recv_in[g, here, :].astype(F32)).astype(BF16)

        def give(j, _):
            s = j + jnp.where(j >= me, 1, 0)
            remote(send_out.at[g, chunk(s)], recv_out.at[g, chunk(me)], ss_out.at[g], rs_out.at[g], s).start()
            return 0

        least = (CH * i + rows - 1) // rows - jnp.where((turn > 0) & (i > 0), 1, 0)
        most = CH * (i + 1) // rows + jnp.where((turn == lanes - 1) & (i < lanes - 1), 1, 0)
        lax.fori_loop(least - jnp.where(least > me, 1, 0), most - jnp.where(most > me, 1, 0), give, 0)

        @pl.when((least <= me) & (me < most))
        def _():
            pltpu.make_async_copy(send_out.at[g, chunk(me)], recv_out.at[g, chunk(me)], rs_out.at[g]).start()

    wait_wave(2, rs_bias)
    start_wave(3)
    prepare(0)
    wait_wave(3, rs_bias)
    lax.fori_loop(1, groups, send_rest, 0)
    def spread_two(p2, _):
        spread_bias(2 * p2, 0)
        spread_bias(2 * p2 + 1, 0)
        return 0

    lax.fori_loop(0, n // 4, spread_two, 0)

    def group(g, _):
        attend(g)

        @pl.when(g < groups - 1)
        def _():
            prepare(g + 1)

        return 0

    lax.fori_loop(0, groups, group, 0)

    for w in range(4):
        wait_wave(w, ss_bias)

    def drain(g, _):
        wait_bytes(recv_out.at[g], rs_out.at[g])
        wait_bytes(send_in.at[g, pl.ds(0, (n - 1) * block)], ss_in.at[g])
        wait_bytes(send_out.at[g, pl.ds(0, (n - 1) * block)], ss_out.at[g])
        return 0

    lax.fori_loop(0, groups, drain, 0)


def collect(received, out, mix):
    rows, wide, _ = out.shape
    top = upper_half((wide // 8, 8, CH))
    mix[...] = received[0].astype(F32).reshape(mix.shape)
    for a in range(0, rows, 2):
        low = mix[:, 0, 4 * a : 4 * a + 8, :]
        high = mix[:, 1, 4 * a : 4 * a + 8, :]
        out[a] = jnp.where(top, low, pltpu.roll(high, 4, 1)).reshape(wide, CH).astype(BF16)
        out[a + 1] = jnp.where(top, pltpu.roll(low, 4, 1), high).reshape(wide, CH).astype(BF16)


def on_device(n, pair_act, ln_gain, ln_shift, w_qkv, w_bias, w_gate, gate_shift, w_out, out_shift):
    rows, full, channels = pair_act.shape
    groups = full // (4 * n)
    block = 4 * rows
    lanes = full // CH
    vmem = pl.BlockSpec(memory_space=pltpu.VMEM)
    dma = pltpu.SemaphoreType.DMA
    received = pl.pallas_call(
        functools.partial(kernel, n),
        out_shape=jax.ShapeDtypeStruct((groups, n * block, CH), BF16),
        in_specs=[vmem] * 9,
        out_specs=pl.BlockSpec(memory_space=pl.ANY),
        scratch_shapes=[
            pltpu.VMEM((groups, n * block, CH), BF16),
            pltpu.VMEM((groups, n * block, CH), BF16),
            pltpu.VMEM((groups, n * block, CH), BF16),
            pltpu.VMEM((4, 4, 2, HEADS * rows, full), BF16),
            pltpu.VMEM((2 * lanes, full, 2 * CH), F32),
            pltpu.VMEM((n // 2, 2, block, CH), F32),
            pltpu.VMEM((n * block, CH), F32),
            pltpu.VMEM((4 * CH, CH), F32),
            pltpu.VMEM((HEADS * rows, full), F32),
            pltpu.VMEM((CH, CH), BF16),
            pltpu.VMEM((2, CH, CH), BF16),
            pltpu.VMEM((CH, CH), BF16),
            pltpu.VMEM((8 * lanes, CH, 2 * CH), BF16),
            pltpu.VMEM((4, 2, full, CH), BF16),
            pltpu.VMEM((4, CH, full), BF16),
            pltpu.VMEM((4, full, CH), F32),
            pltpu.VMEM((2, full, 2 * CH), F32),
            pltpu.VMEM((2, full, 2 * CH), F32),
            pltpu.VMEM((2, 16, 2 * CH), F32),
            pltpu.VMEM((4, lanes, CH, CH), F32),
            dma((16,)), dma((16,)), dma((groups,)), dma((groups,)), dma((groups,)), dma((groups,)),
        ],
        compiler_params=pltpu.CompilerParams(
            collective_id=0, has_side_effects=True, vmem_limit_bytes=56 * 2**20
        ),
        name="triangle",
    )(
        pair_act, ln_gain[None], ln_shift[None], w_qkv, w_bias.T, w_gate, gate_shift[None], w_out, out_shift[None],
    )
    return pl.pallas_call(
        collect,
        grid=(groups,),
        out_shape=jax.ShapeDtypeStruct(pair_act.shape, BF16),
        in_specs=[pl.BlockSpec((1, n * block, CH), lambda g: (g, 0, 0))],
        out_specs=pl.BlockSpec((rows, 4 * n, CH), lambda g: (0, g, 0)),
        scratch_shapes=[pltpu.VMEM((n // 2, 2, block, CH), F32)],
        compiler_params=pltpu.CompilerParams(vmem_limit_bytes=60 * 2**20),
        name="collect",
    )(received)


def solution(mesh):
    in_specs = (P(("dp", "axial"), None, None), P(), P(), P(), P(), P(), P(), P(), P())
    out_specs = P(("dp", "axial"), None, None)
    return jax.shard_map(
        functools.partial(on_device, mesh.shape["axial"]),
        mesh=mesh, in_specs=in_specs, out_specs=out_specs, check_vma=False,
    )
```
